512 devices in a mesh: rep: 64 (over y, z_lo, x), tp: 8 (over z_hi, core).
Axes of the slice: x: 4, y: 4, z: 16 (z_hi: 4, z_lo: 4; z = z_hi * 4 + z_lo), core: 2. Of those that a mesh axis runs over, the one named last changes fastest.
Arguments:
- lookup_vectors: bfloat16 [4, 256, 128, 128], P(None, 'rep', 'tp'), may hold values from -5 to 5
- fresh_token_memory: bfloat16 [4, 256, 2, 8, 128], P(None, 'rep', None, 'tp'), may hold values from -5 to 5
- unfinished_block_memory: bfloat16 [256, 2, 16, 8, 128], P('rep', None, None, 'tp'), may hold values from -5 to 5
- cache_block_store: bfloat16 [4096, 2, 16, 8, 128], P('rep', None, None, 'tp'), may hold values from -7.5 to 7.5
- sequence_block_index: int32 [256, 128], P('rep'), may hold values from 0 to 191
- sequence_history_count: int32 [256], P('rep'), may hold values from 1 to 2048, as said below
- unfinished_block_fill: int32 [256], P('rep'), may hold values from 0 to 12
- migration_sender_block: int32 [4096], P('rep'), may hold values from 0 to 67
- migration_receiver_server: int32 [4096, 1], P('rep'), may hold values from 0 to 63; in each aligned block of 64 rows (0 to 63, 64 to 127, ...) at most 2 rows name the same one
- switch_moment: int32 [256], P('rep'), may hold values from 0 to 4
- output_scaling_weights: float32 [16384], P('tp'), may hold values from 0.5 to 1.5
Outputs:
- normed: bfloat16 [4, 256, 16384], P(None, 'rep', 'tp')
The draws below stay inside these ranges and needn't reach their ends.
Inputs may be any that keep to these rules, and one draw needn't show every extreme that they name: `sequence_block_index`: an entry below 64 names a page of the request's own replica, an entry 64 + j its arrival slot j. `sequence_history_count`: some request holds the full 128 * 16 tokens in every draw. `migration_sender_block`: an entry below 64 names a page of the replica's own pool, an entry 64 + i the tail page of its request i. `migration_receiver_server`: among the 64 entries of one replica no destination appears more than 2 times.
All inputs are finite; a program needn't handle non-finite values.
Results may differ from the reference program's by a relative error of at most 0.0056.
Values may be sent and summed in bfloat16 or wider, within the bound.
No kernel may reach another device: no remote copies, remote signals or barrier semaphores. Data moves between devices by JAX's collectives and lax.ppermute only.
A program may use at most 64 MiB of HBM per device.

```python
import math
import jax
import jax.numpy as jnp
import numpy as np
from jax import lax

H = 128
KVH = 8
HD = 128
PAGE_TOKENS = 16
DECODE_STEP_COUNT = 4
REQ_DEV = 4
PAGES_REQ = 128
POOL_PAGE_COUNT = 64
MIG_DEV = 64
REQS = 256
PAGES_ALL = 4096
MIGS = 4096
CAP = 2
ARRIVE = 128
N_REP = 64


def draw_lookup_vectors(key, part):
    key = jax.random.fold_in(key, 11)
    first = jax.random.fold_in(key, 0)
    shape = (DECODE_STEP_COUNT, REQS, H, HD)
    base = jnp.clip(jax.random.normal(first, shape, jnp.float32), -5.0, 5.0)
    return base.astype(jnp.bfloat16)


def draw_cache_block_store(key, part):
    key = jax.random.fold_in(key, 23)
    first = jax.random.fold_in(key, 0)
    fourth = jax.random.fold_in(key, 3)
    shape = (PAGES_ALL, PAGE_TOKENS, KVH, HD)
    level = jnp.arange(KVH, dtype=jnp.float32)[None, None, :, None] / (KVH - 1)
    keys = jnp.clip(jax.random.normal(first, shape, jnp.float32), -5.0, 5.0)
    values = jnp.clip(jax.random.normal(fourth, shape, jnp.float32), -5.0, 5.0) * 0.5 * jnp.power(3.0, level)
    return jnp.stack([keys, values], axis=1).astype(jnp.bfloat16)


def draw_sequence_history_count(key, part):
    key = jax.random.fold_in(key, 37)
    first, second = jax.random.split(key)
    longest = PAGES_REQ * PAGE_TOKENS
    lengths = jax.random.randint(first, (REQS,), 1, longest + 1)
    full = jax.random.randint(second, (), 0, REQS)
    return jnp.where(jnp.arange(REQS) == full, longest, lengths).astype(jnp.int32)


def touch_ends(array, stream_key, smallest, top_value):
    shape = array.shape
    spot = [jax.random.randint(jax.random.fold_in(stream_key, axis), (), 0, shape[axis]) for axis in range(len(shape))]
    array = array.at[tuple(spot)].set(smallest)
    longest = shape.index(max(shape))
    spot[longest] = (spot[longest] + 1) % shape[longest]
    return array.at[tuple(spot)].set(top_value)


def block_levels(stream_key, dims, shards, low, top_value):
    level, own = 1.0, jax.random.fold_in(stream_key, 6)
    for dim, blocks in shards:
        steps = jnp.exp(jax.random.uniform(jax.random.fold_in(own, dim), (blocks,), jnp.float32, low / len(shards), top_value / len(shards)))
        level = level * jnp.repeat(steps, dims[dim] // blocks).reshape([-1 if axis == dim else 1 for axis in range(len(dims))])
    return level


def routed_block(own_key, own, number, rows, amount, top, limit, lean):
    order = jax.random.permutation(own_key, amount)
    crowded, ordinary = portions_of(amount, rows * top, limit, lean, True), portions_of(amount, rows * top, limit, lean, False)
    places = jnp.arange(amount)

    def named(sizes, rotation):
        used = int((sizes > 0).sum())
        fixed = max(1, used // 4)
        moved = fixed + (places - fixed + rotation * (used - fixed)) % max(1, amount - fixed)
        return jnp.zeros((amount,), jnp.int32).at[order[jnp.where(places < fixed, places, moved)]].set(jnp.asarray(sizes, jnp.int32))

    sizes = jnp.where(number % 4 == 0, named(crowded, number // 4), named(ordinary, number - number // 4 - 1))
    mixed = jax.random.permutation(jax.random.fold_in(own, 3), amount)
    giver, sink = mixed[0:amount // 2 * 2:2], mixed[1:amount // 2 * 2:2]
    margin = jnp.minimum(sizes[giver] - 1, limit - sizes[sink]) // 2
    margin = jnp.where((giver == order[0]) | (sink == order[0]) | (sizes[sink] == 0), 0, jnp.maximum(margin, 0))
    moved = jax.random.randint(jax.random.fold_in(own, 4), (amount // 2,), 0, 1 << 20) % (margin + 1)
    sizes = sizes.at[giver].add(-moved).at[sink].add(moved)
    labels = jnp.searchsorted(jnp.cumsum(sizes), jnp.arange(rows * top), side="right").astype(jnp.int32)
    listing = labels.reshape(top, rows).T
    listing = listing[jax.random.permutation(jax.random.fold_in(own, 1), rows)]
    rotation = jax.random.randint(jax.random.fold_in(own, 2), (rows, 1), 0, top)
    return jnp.take_along_axis(listing, (jnp.arange(top)[None, :] + rotation) % top, axis=1)


def portions_of(count, total, reach, lean, full):
    portions = [(1 << 20) // math.isqrt(rank ** lean) + 1 for rank in range(1, count + 1)]
    largest = reach if full else min(reach, max(-(-total // count), total * portions[0] // sum(portions)))
    least = 1 if total - largest >= count - 1 else 0
    counts, spare = [largest] + [least] * (count - 1), total - largest - least * (count - 1)
    while spare > 0:
        candidates = [i for i in range(1, count) if counts[i] < largest] or [i for i in range(1, count) if counts[i] < reach]
        pool, remaining = sum([portions[i] for i in candidates]), spare
        for i in candidates:
            addition = min(reach - counts[i], max(1, remaining * portions[i] // pool), spare)
            counts[i] = counts[i] + addition
            spare = spare - addition
    return np.array(counts)


def scatter_about(own_key, dims, scale, limit, cuts=(), kind=jnp.bfloat16):
    gain = block_levels(own_key, dims, cuts, -0.22, 0.18) if cuts else 1.0
    values = jax.random.normal(own_key, dims, jnp.float32) * scale * gain
    return jnp.minimum(jnp.maximum(values, -limit), limit).astype(kind)


def setup_inputs(seed: int = 0) -> dict:
    key_list = jax.random.split(jax.random.key(seed), 12)
    lookup_vectors = draw_lookup_vectors(jax.random.fold_in(key_list[11], 71), 0)
    fresh_token_memory = scatter_about(key_list[1], (DECODE_STEP_COUNT, REQS, 2, KVH, HD), 1.0, 5.0, ((1, 64), (3, 8)))
    unfinished_block_memory = scatter_about(key_list[2], (REQS, 2, PAGE_TOKENS, KVH, HD), 1.0, 5.0, ((0, 64), (3, 8)))
    cache_block_store = draw_cache_block_store(jax.random.fold_in(key_list[11], 71), 0)
    sequence_block_index = touch_ends(jax.random.randint(key_list[4], (REQS, PAGES_REQ), 0, POOL_PAGE_COUNT + ARRIVE), jax.random.fold_in(key_list[4], 1), 0, (POOL_PAGE_COUNT + ARRIVE) - 1).astype(jnp.int32)
    sequence_history_count = draw_sequence_history_count(jax.random.fold_in(key_list[11], 71), 0)
    unfinished_block_fill = touch_ends(jax.random.randint(key_list[6], (REQS,), 0, PAGE_TOKENS - DECODE_STEP_COUNT + 1), jax.random.fold_in(key_list[6], 1), 0, PAGE_TOKENS - DECODE_STEP_COUNT).astype(jnp.int32)
    migration_sender_block = touch_ends(jax.random.randint(key_list[7], (MIGS,), 0, POOL_PAGE_COUNT + REQ_DEV), jax.random.fold_in(key_list[7], 1), 0, (POOL_PAGE_COUNT + REQ_DEV) - 1).astype(jnp.int32)
    migration_receiver_server_keys = jax.random.split(jax.random.fold_in(key_list[8], 1), MIGS // MIG_DEV)
    migration_receiver_server_turns = jax.random.permutation(jax.random.fold_in(key_list[8], 3), MIGS // MIG_DEV)
    migration_receiver_server = jax.vmap(lambda own, number: routed_block(jax.random.fold_in(key_list[8], 2), own, number, MIG_DEV, N_REP, 1, CAP, 2))(migration_receiver_server_keys, migration_receiver_server_turns).reshape((MIGS, 1))
    switch_moment = touch_ends(jax.random.randint(key_list[9], (REQS,), 0, DECODE_STEP_COUNT + 1), jax.random.fold_in(key_list[9], 1), 0, DECODE_STEP_COUNT).astype(jnp.int32)
    output_scaling_weights = jnp.clip(1.0 + 0.1 * jax.random.normal(key_list[10], (H * HD,), jnp.float32), 0.5, 1.5)
    return dict(lookup_vectors=lookup_vectors, fresh_token_memory=fresh_token_memory, unfinished_block_memory=unfinished_block_memory, cache_block_store=cache_block_store, sequence_block_index=sequence_block_index, sequence_history_count=sequence_history_count, unfinished_block_fill=unfinished_block_fill, migration_sender_block=migration_sender_block, migration_receiver_server=migration_receiver_server, switch_moment=switch_moment, output_scaling_weights=output_scaling_weights)


def filled_tail(unfinished_block_memory, fresh_token_memory, unfinished_block_fill):
    decode_steps = fresh_token_memory.shape[0]
    page_entry = unfinished_block_memory.shape[2]
    offsets = jnp.arange(page_entry, dtype=jnp.int32)
    hits = offsets[None, None, :] == unfinished_block_fill[None, :, None] + jnp.arange(decode_steps, dtype=jnp.int32)[:, None, None]
    placed = jnp.einsum('srp,srckd->rcpkd', hits.astype(jnp.float32), fresh_token_memory.astype(jnp.float32))
    covered = jnp.any(hits, axis=0)
    merged = jnp.where(covered[:, None, :, None, None], placed, unfinished_block_memory.astype(jnp.float32))
    return merged.astype(jnp.bfloat16)

def slot_ranks(target):
    order = jnp.arange(target.shape[0], dtype=jnp.int32)
    same = (target[:, None] == target[None, :]) & (order[None, :] < order[:, None])
    return lax.optimization_barrier(jnp.sum(same.astype(jnp.int32), axis=1, dtype=jnp.int32))

def token_validity(page_table_row, context_length, arrival_length, tail_length, boundary_marker, pool_page_tiles, page_entry, decode_steps):
    entry = jnp.repeat(page_table_row, page_entry)
    position = jnp.arange(entry.shape[0], dtype=jnp.int32)
    offset = position % page_entry
    incoming = entry >= pool_page_tiles
    known = arrival_length[jnp.clip(entry - pool_page_tiles, 0, arrival_length.shape[0] - 1)]
    step = jnp.arange(decode_steps, dtype=jnp.int32)[:, None]
    page_ok = (position < context_length)[None, :] & (jnp.logical_not(incoming)[None, :] | (step >= boundary_marker) & (offset < known)[None, :])
    tail_ok = jnp.arange(page_entry, dtype=jnp.int32)[None, :] < tail_length + step + 1
    return jnp.concatenate([page_ok, tail_ok], axis=1)

def attend(query_vector, pages, tail_block, valid_mask):
    decode_steps, heads, hdim = query_vector.shape
    kv_heads = pages.shape[3]
    keys = jnp.concatenate([pages[:, 0].reshape(-1, kv_heads, hdim), tail_block[0]], 0)
    values = jnp.concatenate([pages[:, 1].reshape(-1, kv_heads, hdim), tail_block[1]], 0)
    grouped = query_vector.reshape(decode_steps, kv_heads, heads // kv_heads, hdim)
    scores = jnp.einsum('skgd,lkd->skgl', grouped.astype(jnp.float32), keys.astype(jnp.float32)) / math.sqrt(hdim)
    scores = jnp.where(valid_mask[:, None, None, :], scores, -jnp.inf)
    top = lax.optimization_barrier(jnp.max(scores, axis=-1, keepdims=True))
    probs = jnp.exp(scores - top)
    total = lax.optimization_barrier(jnp.sum(probs, axis=-1, keepdims=True))
    weights = probs.astype(jnp.bfloat16)
    mixed = jnp.einsum('skgl,lkd->skgd', weights.astype(jnp.float32), values.astype(jnp.float32)) / total
    return mixed.reshape(decode_steps, heads, hdim).astype(jnp.bfloat16)

def reference(lookup_vectors, fresh_token_memory, unfinished_block_memory, cache_block_store, sequence_block_index, sequence_history_count, unfinished_block_fill, migration_sender_block, migration_receiver_server, switch_moment, output_scaling_weights):
    tails = filled_tail(unfinished_block_memory, fresh_token_memory, unfinished_block_fill)
    source = migration_sender_block.reshape(N_REP, MIG_DEV)
    target = migration_receiver_server.reshape(N_REP, MIG_DEV)
    ranks = jax.vmap(slot_ranks)(target)
    anchor = jnp.arange(N_REP, dtype=jnp.int32)[:, None]
    landing = (target * ARRIVE + anchor * CAP + ranks).reshape(-1)
    from_tail = (source >= POOL_PAGE_COUNT).reshape(-1)
    pool_pick = (anchor * POOL_PAGE_COUNT + jnp.clip(source, 0, POOL_PAGE_COUNT - 1)).reshape(-1)
    tail_pick = (anchor * REQ_DEV + jnp.clip(source - POOL_PAGE_COUNT, 0, REQ_DEV - 1)).reshape(-1)
    lengths = jnp.where(from_tail, unfinished_block_fill[tail_pick] + switch_moment[tail_pick], PAGE_TOKENS).astype(jnp.int32)
    slots = N_REP * ARRIVE
    slot_pool = jnp.zeros((slots,), jnp.int32).at[landing].set(pool_pick.astype(jnp.int32))
    slot_tail = jnp.zeros((slots,), jnp.int32).at[landing].set(tail_pick.astype(jnp.int32))
    slot_flag = jnp.zeros((slots,), jnp.int32).at[landing].set(from_tail.astype(jnp.int32))
    slot_len = jnp.zeros((slots,), jnp.int32).at[landing].set(lengths)

    def one_replica(replica):
        start = (replica * ARRIVE).astype(jnp.int32)
        pick_pool = lax.dynamic_slice_in_dim(slot_pool, start, ARRIVE)
        pick_tail = lax.dynamic_slice_in_dim(slot_tail, start, ARRIVE)
        pick_flag = lax.dynamic_slice_in_dim(slot_flag, start, ARRIVE)
        selected_length = lax.dynamic_slice_in_dim(slot_len, start, ARRIVE)
        arrivals = jnp.where((pick_flag > 0)[:, None, None, None, None], tails[pick_tail], cache_block_store[pick_pool])
        arrivals = jnp.where((selected_length > 0)[:, None, None, None, None], arrivals, jnp.zeros_like(arrivals))
        own = lax.dynamic_slice_in_dim(cache_block_store, (replica * POOL_PAGE_COUNT).astype(jnp.int32), POOL_PAGE_COUNT)
        extended = jnp.concatenate([own, arrivals], 0)
        first = (replica * REQ_DEV).astype(jnp.int32)
        rows_query = lax.dynamic_slice_in_dim(lookup_vectors, first, REQ_DEV, 1)
        rows_table = lax.dynamic_slice_in_dim(sequence_block_index, first, REQ_DEV)
        rows_tail = lax.dynamic_slice_in_dim(tails, first, REQ_DEV)
        rows_ctx = lax.dynamic_slice_in_dim(sequence_history_count, first, REQ_DEV)
        rows_tlen = lax.dynamic_slice_in_dim(unfinished_block_fill, first, REQ_DEV)
        rows_switch = lax.dynamic_slice_in_dim(switch_moment, first, REQ_DEV)

        def one_request(request_element):
            query_vector, page_table_row, tail_block, context_length, tail_length, handover_step = request_element
            valid_mask = token_validity(page_table_row, context_length, selected_length, tail_length, handover_step, POOL_PAGE_COUNT, PAGE_TOKENS, DECODE_STEP_COUNT)
            return attend(query_vector, extended[page_table_row], tail_block, valid_mask)
        return lax.map(one_request, (jnp.transpose(rows_query, (1, 0, 2, 3)), rows_table, rows_tail, rows_ctx, rows_tlen, rows_switch))
    mixed = lax.map(one_replica, jnp.arange(N_REP, dtype=jnp.int32))
    attn = jnp.transpose(mixed.reshape(REQS, DECODE_STEP_COUNT, H * HD), (1, 0, 2))
    wide = attn.astype(jnp.float32)
    mean = lax.optimization_barrier(jnp.sum(wide * wide, axis=-1, keepdims=True)) / (H * HD)
    return (wide * lax.rsqrt(mean + 1e-05) * output_scaling_weights).astype(jnp.bfloat16)
```

```python
import jax
import jax.numpy as jnp
from jax import lax
from jax.experimental import pallas as pl
from jax.experimental.pallas import tpu as pltpu
from jax.sharding import PartitionSpec as P

STEPS, REQS, HEADS, HD = 4, 4, 16, 128
ROWS = STEPS * REQS * HEADS
PAIRS = STEPS * REQS
PAGE = 16
POOL = 64
MIGS = 64
PEERS = 32
TOKENS = POOL * PAGE
NEG = -1e30
MARK = 4096.0
SCALE = 1.4426950408889634 / HD**0.5
F32, BF16, I32 = jnp.float32, jnp.bfloat16, jnp.int32
VMEM = pl.BlockSpec(memory_space=pltpu.VMEM)
SMEM = pl.BlockSpec(memory_space=pltpu.SMEM)


def dot(a, b, ca, cb):
    return lax.dot_general(a, b, (((ca,), (cb,)), ((), ())), preferred_element_type=F32)


def iota(shape, axis):
    return lax.broadcasted_iota(I32, shape, axis)


def tail_tile(r, kv, fill, unfinished_ref, fresh_ref):
    rows = iota((PAGE, HD), 0)
    tile = unfinished_ref[r, kv * PAGE : (kv + 1) * PAGE, :].astype(F32)
    for s in range(STEPS):
        row = fresh_ref[s, r].astype(F32)[kv : kv + 1, :]
        tile = jnp.where(rows == fill + s, row, tile)
    return tile


def send_kernel(half_ref, target_ref, source_ref, fill_ref, switch_ref, pool_ref, unfinished_ref, fresh_ref, out_ref, cut_ref):
    rows = iota((PAGE, HD), 0)
    blank = jnp.concatenate([jnp.full((PAGE, HD), MARK, BF16), jnp.zeros((PAGE, HD), BF16)], 0)
    out_ref[...] = jnp.broadcast_to(blank[None], out_ref.shape)
    for r in range(REQS):
        fill = fill_ref[r]
        key = tail_tile(r, 0, fill, unfinished_ref, fresh_ref)
        value = tail_tile(r, 1, fill, unfinished_ref, fresh_ref)
        key = jnp.where(rows < fill + switch_ref[r], key, MARK)
        cut_ref[r] = jnp.concatenate([key, value], 0).astype(BF16)
    half = half_ref[0]
    low = jnp.int32(0)
    high = jnp.int32(0)
    for e in range(MIGS):
        t = target_ref[e]
        m = source_ref[e]
        first = t < 32
        shift = t & 31
        word = jnp.where(first, low, high)
        rank = (word >> shift) & 1
        word = word | (jnp.int32(1) << shift)
        low = jnp.where(first, word, low)
        high = jnp.where(first, high, word)
        peer = ((t >> 4) << 3) | (t & 7)
        which = ((t >> 3) & 1) ^ half
        slot = peer * 4 + which * 2 + rank
        pooled = pool_ref[jnp.minimum(m, POOL - 1)]
        cut = cut_ref[jnp.maximum(m - POOL, 0)]
        out_ref[slot] = jnp.where(m < POOL, pooled, cut)


def send_tiles(half, target, source, fill, switch, pool, unfinished, fresh):
    return pl.pallas_call(
        send_kernel,
        out_shape=jax.ShapeDtypeStruct((PEERS * 4, 2 * PAGE, HD), BF16),
        in_specs=[SMEM] * 5 + [VMEM] * 3,
        out_specs=VMEM,
        scratch_shapes=[pltpu.VMEM((REQS, 2 * PAGE, HD), BF16)],
        cost_estimate=pl.CostEstimate(flops=1000, bytes_accessed=2**21, transcendentals=0),
        name="send_tiles",
    )(half, target, source, fill, switch, pool, unfinished, fresh)


def count_kernel(half_ref, length_ref, switch_ref, table_ref, pool_ref, near_ref, far_ref):
    half = half_ref[0]
    offset = iota((PAGE, HD), 0)
    position = iota((PAGE, HD), 1) * PAGE + offset
    slot = iota((POOL, HD), 0)
    spread = (iota((POOL, TOKENS), 1) // PAGE == iota((POOL, TOKENS), 0)).astype(BF16)
    own = iota((POOL, TOKENS), 1) % PAGE == iota((POOL, TOKENS), 0) % PAGE
    fold = (iota((PAIRS, POOL), 1) // PAGE == iota((PAIRS, POOL), 0) % REQS).astype(BF16)
    pair = iota((PAIRS, TOKENS), 0)
    step, req = pair // REQS, pair % REQS
    moment = jnp.zeros((PAIRS, TOKENS), I32)
    for g in range(REQS):
        moment = jnp.where(req == g, switch_ref[g], moment)
    for section, ref in ((0, pool_ref), (1, near_ref), (2, far_ref)):
        if section == 0:
            page = slot
        else:
            side = half if section == 1 else 1 - half
            page = POOL + (slot // 16) * 32 + side * 16 + slot % 16
        counts = []
        for g in range(REQS):
            valid = (position < length_ref[g]).astype(BF16)
            hit = (table_ref[g : g + 1, :] == page).astype(BF16)
            counts.append(dot(valid, hit, 1, 1))
        counts = jnp.concatenate(counts, 0).astype(BF16)
        wide = jnp.where(own, dot(counts, spread, 1, 0), 0.0).astype(BF16)
        wide = dot(fold, wide, 1, 0)
        if section:
            wide = jnp.where(step >= moment, wide, 0.0)
        ref[...] = wide.astype(BF16)


def count_tokens(half, length, switch, table):
    shape = jax.ShapeDtypeStruct((PAIRS, TOKENS), BF16)
    return pl.pallas_call(
        count_kernel,
        out_shape=(shape,) * 3,
        in_specs=[SMEM] * 3 + [VMEM],
        out_specs=(VMEM,) * 3,
        cost_estimate=pl.CostEstimate(flops=2**27, bytes_accessed=2**18, transcendentals=0),
        name="count_tokens",
    )(half, length, switch, table)


def bias_of(count):
    count = count.astype(F32)
    return jnp.where(count > 0, jnp.log2(jnp.maximum(count, 1.0)), NEG)


def attend(query, key, value, bias, probs_ref):
    scores = dot(query, key, 1, 1)
    width = key.shape[0]
    logs, sums = [], []
    for h in range(HEADS):
        rows = slice(h * PAIRS, (h + 1) * PAIRS)
        x = scores[rows] * SCALE + bias
        top = jnp.max(x, axis=-1, keepdims=True)
        p = jnp.exp2(x - top)
        total = jnp.sum(p, axis=-1, keepdims=True)
        probs_ref[rows, :width] = p.astype(BF16)
        logs.append(top + jnp.log2(total))
        sums.append(total)
    mixed = dot(probs_ref[:, :width], value, 1, 0) / jnp.concatenate(sums, 0)
    return mixed, jnp.concatenate(logs, 0)


def combine(a, b):
    (x, p), (y, q) = a, b
    top = jnp.maximum(p, q)
    u, v = jnp.exp2(p - top), jnp.exp2(q - top)
    return (x * u + y * v) / (u + v), top + jnp.log2(u + v)


def local_kernel(fill_ref, query_ref, pool_ref, unfinished_ref, fresh_ref, count_ref, mixed_ref, log_ref, probs_ref):
    query = query_ref[...]
    key = pool_ref[:, :PAGE, :].reshape(TOKENS, HD)
    value = pool_ref[:, PAGE:, :].reshape(TOKENS, HD)
    part = attend(query, key, value, bias_of(count_ref[...]), probs_ref)
    tail = REQS * PAGE
    keys, values = [], []
    pair, lane = iota((PAIRS, tail), 0), iota((PAIRS, tail), 1)
    step, req = pair // REQS, pair % REQS
    held = jnp.zeros((PAIRS, tail), I32)
    for r in range(REQS):
        fill = fill_ref[r]
        keys.append(tail_tile(r, 0, fill, unfinished_ref, fresh_ref))
        values.append(tail_tile(r, 1, fill, unfinished_ref, fresh_ref))
        held = jnp.where(req == r, fill, held)
    valid = (lane // PAGE == req) & (lane % PAGE < held + step + 1)
    keys = jnp.concatenate(keys, 0).astype(BF16)
    values = jnp.concatenate(values, 0).astype(BF16)
    tails = attend(query, keys, values, jnp.where(valid, 0.0, NEG), probs_ref)
    mixed, log = combine(part, tails)
    mixed_ref[...] = mixed
    log_ref[...] = jnp.broadcast_to(log, log_ref.shape)


def local_part(fill, query, pool, unfinished, fresh, count):
    shape = jax.ShapeDtypeStruct((ROWS, HD), F32)
    return pl.pallas_call(
        local_kernel,
        out_shape=(shape, shape),
        in_specs=[SMEM] + [VMEM] * 5,
        out_specs=(VMEM, VMEM),
        scratch_shapes=[pltpu.VMEM((ROWS, TOKENS), BF16)],
        cost_estimate=pl.CostEstimate(flops=2**28, bytes_accessed=2**20, transcendentals=2**18),
        name="local_part",
    )(fill, query, pool, unfinished, fresh, count)


def arrived_part(query, count, tiles_ref, which, probs_ref):
    tiles = tiles_ref[:, 2 * which : 2 * which + 2]
    key = tiles[:, :, :PAGE, :].reshape(TOKENS, HD)
    value = tiles[:, :, PAGE:, :].reshape(TOKENS, HD)
    pick = (iota((PAIRS, HD), 1) == 0).astype(BF16)
    there = dot(pick, key, 1, 1) < MARK / 2
    bias = jnp.where(there, bias_of(count), NEG)
    return attend(query, key, value, bias, probs_ref)


def far_kernel(request_ref, tiles_ref, out_ref, probs_ref):
    query = request_ref[:ROWS, :]
    count = jnp.concatenate([request_ref[ROWS + PAIRS * i : ROWS + PAIRS * (i + 1), :] for i in range(TOKENS // HD)], 1)
    mixed, log = arrived_part(query, count, tiles_ref, 1, probs_ref)
    out_ref[:ROWS, :] = mixed.astype(BF16)
    lane = iota((ROWS, HD), 1)
    high = log.astype(BF16).astype(F32)
    middle = (log - high).astype(BF16).astype(F32)
    least = log - high - middle
    parts = jnp.where(lane == 0, high, jnp.where(lane == 1, middle, jnp.where(lane == 2, least, 0.0)))
    eye = (iota((8, HD), 0) == iota((8, HD), 1)).astype(BF16)
    across = dot(eye, parts.astype(BF16), 1, 1)
    out_ref[ROWS:, :] = jnp.concatenate([across[:, :HD], across[:, HD:]], 0).astype(BF16)


def far_part(request, tiles):
    return pl.pallas_call(
        far_kernel,
        out_shape=jax.ShapeDtypeStruct((ROWS + 16, HD), BF16),
        in_specs=[VMEM, VMEM],
        out_specs=VMEM,
        scratch_shapes=[pltpu.VMEM((ROWS, TOKENS), BF16)],
        cost_estimate=pl.CostEstimate(flops=2**28, bytes_accessed=2**20, transcendentals=2**18),
        name="far_part",
    )(request, tiles)


def near_kernel(query_ref, count_ref, tiles_ref, mixed_ref, log_ref, out_ref, sum_ref, probs_ref):
    part = arrived_part(query_ref[...], count_ref[...], tiles_ref, 0, probs_ref)
    mixed, log = combine((mixed_ref[...], log_ref[...]), part)
    out_ref[...] = mixed
    sum_ref[...] = log


def near_part(query, count, tiles, mixed, log):
    shape = jax.ShapeDtypeStruct((ROWS, HD), F32)
    return pl.pallas_call(
        near_kernel,
        out_shape=(shape, shape),
        in_specs=[VMEM] * 5,
        out_specs=(VMEM, VMEM),
        scratch_shapes=[pltpu.VMEM((ROWS, TOKENS), BF16)],
        cost_estimate=pl.CostEstimate(flops=2**28, bytes_accessed=2**20, transcendentals=2**18),
        name="near_part",
    )(query, count, tiles, mixed, log)


def merge_kernel(mixed_ref, log_ref, back_ref, attn_ref, square_ref):
    stats = back_ref[ROWS:, :].astype(F32)
    stats = jnp.concatenate([stats[:8], stats[8:]], 1).astype(BF16)
    log = dot(stats, jnp.ones((8, HD), BF16), 0, 0)
    mixed, _ = combine((mixed_ref[...], log_ref[...]), (back_ref[:ROWS, :].astype(F32), log))
    attn = mixed.astype(BF16)
    attn_ref[...] = attn
    wide = attn.astype(F32)
    square = wide * wide
    total = square[:PAIRS]
    for h in range(1, HEADS):
        total = total + square[h * PAIRS : (h + 1) * PAIRS]
    total = jnp.sum(total, axis=-1, keepdims=True)
    line = jnp.sum(jnp.where(iota((PAIRS, HD), 0) == iota((PAIRS, HD), 1), total, 0.0), axis=0, keepdims=True)
    square_ref[...] = jnp.broadcast_to(line[None], square_ref.shape)


def merge(mixed, log, back, ways):
    return pl.pallas_call(
        merge_kernel,
        out_shape=(jax.ShapeDtypeStruct((ROWS, HD), BF16), jax.ShapeDtypeStruct((ways, 1, HD), F32)),
        in_specs=[VMEM] * 3,
        out_specs=(VMEM, VMEM),
        name="merge",
    )(mixed, log, back)


def norm_kernel(attn_ref, square_ref, gain_ref, out_ref):
    ways = square_ref.shape[0]
    line = square_ref[0]
    for i in range(1, ways):
        line = line + square_ref[i]
    line = jnp.broadcast_to(line, (PAIRS, HD))
    total = jnp.sum(jnp.where(iota((PAIRS, HD), 0) == iota((PAIRS, HD), 1), line, 0.0), axis=1, keepdims=True)
    scale = lax.rsqrt(total / (ways * HEADS * HD) + 1e-5)
    for h in range(HEADS):
        wide = attn_ref[h * PAIRS : (h + 1) * PAIRS, :].astype(F32)
        out = wide * scale * gain_ref[h : h + 1, :]
        for t in range(STEPS):
            out_ref[t, :, h * HD : (h + 1) * HD] = out[t * REQS : (t + 1) * REQS].astype(BF16)


def normalize(attn, square, gain):
    return pl.pallas_call(
        norm_kernel,
        out_shape=jax.ShapeDtypeStruct((STEPS, REQS, HEADS * HD), BF16),
        in_specs=[VMEM] * 3,
        out_specs=VMEM,
        name="normalize",
    )(attn, square, gain)


def body(
    lookup_vectors,
    fresh_token_memory,
    unfinished_block_memory,
    cache_block_store,
    sequence_block_index,
    sequence_history_count,
    unfinished_block_fill,
    migration_sender_block,
    migration_receiver_server,
    switch_moment,
    output_scaling_weights,
):
    ways = lax.axis_size("tp")
    half = lax.axis_index("zh").astype(I32).reshape(1)
    pool = cache_block_store.reshape(POOL, 2 * PAGE, HD)
    unfinished = unfinished_block_memory.reshape(REQS, 2 * PAGE, HD)
    fresh = fresh_token_memory.reshape(STEPS, REQS, 2, HD)
    gain = output_scaling_weights.reshape(HEADS, HD)
    fill, switch = unfinished_block_fill, switch_moment

    outgoing = send_tiles(
        half, migration_receiver_server.reshape(MIGS), migration_sender_block, fill, switch, pool, unfinished, fresh
    )
    tiles = lax.all_to_all(outgoing, ("y", "zl", "x"), split_axis=0, concat_axis=0, tiled=True)
    tiles = tiles.reshape(PEERS, 4, 2 * PAGE, HD)

    query = jnp.transpose(lookup_vectors, (2, 0, 1, 3)).reshape(ROWS, HD)
    pool_count, near_count, far_count = count_tokens(half, sequence_history_count, switch, sequence_block_index)
    far_rows = far_count.reshape(PAIRS, TOKENS // HD, HD).transpose(1, 0, 2).reshape(PAIRS * TOKENS // HD, HD)
    request = lax.ppermute(jnp.concatenate([query, far_rows], 0), "zh", [(0, 1), (1, 0)])
    mixed, log = local_part(fill, query, pool, unfinished, fresh, pool_count)

    back = lax.ppermute(far_part(request, tiles), "zh", [(0, 1), (1, 0)])
    mixed, log = near_part(query, near_count, tiles, mixed, log)
    attn, square = merge(mixed, log, back, ways)
    square = lax.all_to_all(square, "tp", split_axis=0, concat_axis=0, tiled=True)
    return normalize(attn, square, gain)


def solution(mesh):
    devices = mesh.devices.reshape(4, 2, 2, 4, mesh.devices.shape[1])
    fine = jax.sharding.Mesh(devices, ("y", "zh", "zl", "x", "tp"))
    rep = ("y", "zh", "zl", "x")
    placed = (
        P(None, rep, "tp", None),
        P(None, rep, None, "tp", None),
        P(rep, None, None, "tp", None),
        P(rep, None, None, "tp", None),
        P(rep, None),
        P(rep),
        P(rep),
        P(rep),
        P(rep, None),
        P(rep),
        P("tp"),
    )
    return jax.shard_map(body, mesh=fine, in_specs=placed, out_specs=P(None, rep, "tp"), check_vma=False)
```

```python
import jax
import jax.numpy as jnp
from jax import lax
from jax.experimental import pallas as pl
from jax.experimental.pallas import tpu as pltpu
from jax.sharding import PartitionSpec as P

STEPS, REQS, HEADS, HD = 4, 4, 16, 128
ROWS = STEPS * REQS * HEADS
PAIRS = STEPS * REQS
PAGE = 16
POOL = 64
MIGS = 64
PEERS = 32
TOKENS = POOL * PAGE
NEG = -1e30
MARK = 4096.0
SCALE = 1.4426950408889634 / HD**0.5
F32, BF16, I32 = jnp.float32, jnp.bfloat16, jnp.int32
VMEM = pl.BlockSpec(memory_space=pltpu.VMEM)
SMEM = pl.BlockSpec(memory_space=pltpu.SMEM)


def dot(a, b, ca, cb):
    return lax.dot_general(a, b, (((ca,), (cb,)), ((), ())), preferred_element_type=F32)


def iota(shape, axis):
    return lax.broadcasted_iota(I32, shape, axis)


def tail_tile(r, kv, fill, unfinished_ref, fresh_ref):
    rows = iota((PAGE, HD), 0)
    tile = unfinished_ref[r, kv * PAGE : (kv + 1) * PAGE, :].astype(F32)
    for s in range(STEPS):
        row = fresh_ref[s, r].astype(F32)[kv : kv + 1, :]
        tile = jnp.where(rows == fill + s, row, tile)
    return tile


def send_kernel(half_ref, target_ref, source_ref, fill_ref, switch_ref, pool_ref, unfinished_ref, fresh_ref, out_ref, cut_ref):
    rows = iota((PAGE, HD), 0)
    blank = jnp.concatenate([jnp.full((PAGE, HD), MARK, BF16), jnp.zeros((PAGE, HD), BF16)], 0)
    out_ref[...] = jnp.broadcast_to(blank[None], out_ref.shape)
    for r in range(REQS):
        fill = fill_ref[r]
        key = tail_tile(r, 0, fill, unfinished_ref, fresh_ref)
        value = tail_tile(r, 1, fill, unfinished_ref, fresh_ref)
        key = jnp.where(rows < fill + switch_ref[r], key, MARK)
        cut_ref[r] = jnp.concatenate([key, value], 0).astype(BF16)
    half = half_ref[0]
    low = jnp.int32(0)
    high = jnp.int32(0)
    for e in range(MIGS):
        t = target_ref[e]
        m = source_ref[e]
        first = t < 32
        shift = t & 31
        word = jnp.where(first, low, high)
        rank = (word >> shift) & 1
        word = word | (jnp.int32(1) << shift)
        low = jnp.where(first, word, low)
        high = jnp.where(first, high, word)
        peer = ((t >> 4) << 3) | (t & 7)
        which = ((t >> 3) & 1) ^ half
        slot = peer * 4 + which * 2 + rank
        pooled = pool_ref[jnp.minimum(m, POOL - 1)]
        cut = cut_ref[jnp.maximum(m - POOL, 0)]
        out_ref[slot] = jnp.where(m < POOL, pooled, cut)


def keep(*arrays):
    return tuple(pltpu.with_memory_space_constraint(x, pltpu.VMEM) for x in arrays)


def send_tiles(half, target, source, fill, switch, pool, unfinished, fresh):
    return pl.pallas_call(
        send_kernel,
        out_shape=pltpu.VMEM((PEERS * 4, 2 * PAGE, HD), BF16),
        in_specs=[SMEM] * 5 + [VMEM] * 3,
        out_specs=VMEM,
        scratch_shapes=[pltpu.VMEM((REQS, 2 * PAGE, HD), BF16)],
        cost_estimate=pl.CostEstimate(flops=1000, bytes_accessed=2**21, transcendentals=0),
        name="send_tiles",
    )(half, target, source, fill, switch, pool, unfinished, fresh)


def request_kernel(length_ref, switch_ref, query_ref, table_ref, out_ref):
    out_ref[:ROWS, :] = query_ref[...]
    row, lane = iota((16, HD), 0), iota((16, HD), 1)
    info = jnp.concatenate([table_ref[...], jnp.zeros((16 - REQS, HD), I32)], 0)
    for g in range(REQS):
        length = length_ref[g]
        at = row - REQS
        fact = jnp.where(at == 0, length >> 4, jnp.where(at == 1, length & 15, switch_ref[g]))
        info = jnp.where((lane == g) & (at >= 0) & (at < 3), fact, info)
    out_ref[ROWS:, :] = info.astype(F32).astype(BF16)


def request_rows(length, switch, query, table):
    return pl.pallas_call(
        request_kernel,
        out_shape=pltpu.VMEM((ROWS + 16, HD), BF16),
        in_specs=[SMEM] * 2 + [VMEM] * 2,
        out_specs=VMEM,
        cost_estimate=pl.CostEstimate(flops=1000, bytes_accessed=2**17, transcendentals=0),
        name="request_rows",
    )(length, switch, query, table)


def bias_kernel(sections, half_ref, request_ref, *refs):
    info = request_ref[ROWS:, :].astype(F32).astype(I32)
    half = half_ref[0]
    token = iota((TOKENS, HD), 0)
    entry = iota((TOKENS, HD), 1)
    place, offset = token // PAGE, token % PAGE
    lane = iota((1, HD), 1)
    pair, part = lane % PAIRS, lane // PAIRS
    step, req = pair // REQS, pair % REQS
    inside, weights = [], []
    late = jnp.zeros((1, HD), jnp.bool_)
    for g in range(REQS):
        pages, rest, moment = (info[REQS + i : REQS + i + 1, g : g + 1] for i in range(3))
        inside.append(entry * PAGE + offset < pages * PAGE + rest)
        late = late | ((req == g) & (step < moment))
        spread = iota((HD, HD), 1)
        weights.append(((spread % REQS == g) & (spread < 3 * PAIRS)).astype(BF16))
    weights = jnp.concatenate(weights, 0)
    for section, ref in zip(sections, refs, strict=True):
        if section == "pool":
            page = place
        else:
            page = POOL + (place // 16) * 32 + half * 16 + place % 16
        hits = [jnp.where((info[g : g + 1, :] == page) & inside[g], 1.0, 0.0).astype(BF16) for g in range(REQS)]
        count = dot(jnp.concatenate(hits, 1), weights, 1, 0)
        log = jnp.log2(jnp.maximum(count, 1.0)) / SCALE
        high = log.astype(BF16).astype(F32)
        middle = (log - high).astype(BF16).astype(F32)
        parts = jnp.where(part == 0, high, jnp.where(part == 1, middle, log - high - middle))
        gone = count == 0
        if section != "pool":
            gone = gone | late
        ref[...] = jnp.where(gone, jnp.where(part == 0, NEG, 0.0), parts).astype(BF16)


def token_bias(sections, half, request):
    out = pltpu.VMEM((TOKENS, HD), BF16)
    return pl.pallas_call(
        lambda *refs: bias_kernel(sections, *refs),
        out_shape=(out,) * len(sections),
        in_specs=[SMEM, VMEM],
        out_specs=(VMEM,) * len(sections),
        cost_estimate=pl.CostEstimate(flops=2**27, bytes_accessed=2**18, transcendentals=0),
        name="token_bias",
    )(half, *keep(request))


def attend(query, key, value, bias):
    lane, row = iota((ROWS, HD), 1), iota((ROWS, HD), 0)
    reads = ((lane % PAIRS == row % PAIRS) & (lane < 3 * PAIRS)).astype(BF16)
    scores = dot(jnp.concatenate([query, reads], 1), jnp.concatenate([key, bias], 1), 1, 1)
    top = jnp.max(scores, axis=-1, keepdims=True)
    probs = jnp.exp2((scores - top) * SCALE).astype(BF16)
    mixed = dot(probs, jnp.concatenate([value, jnp.ones(value.shape, BF16)], 1), 1, 0)
    total = mixed[:, HD:]
    return mixed[:, :HD] / total, top * SCALE + jnp.log2(total)


def combine(a, b):
    (x, p), (y, q) = a, b
    top = jnp.maximum(p, q)
    u, v = jnp.exp2(p - top), jnp.exp2(q - top)
    return (x * u + y * v) / (u + v), top + jnp.log2(u + v)


def local_kernel(fill_ref, request_ref, pool_ref, unfinished_ref, fresh_ref, bias_ref, mixed_ref, log_ref):
    tail = 2 * REQS * PAGE
    keys = [pool_ref[:, :PAGE, :].reshape(TOKENS, HD)]
    values = [pool_ref[:, PAGE:, :].reshape(TOKENS, HD)]
    token, lane = iota((tail, HD), 0), iota((tail, HD), 1)
    step, req = lane % PAIRS // REQS, lane % REQS
    held = jnp.zeros((tail, HD), I32)
    for r in range(REQS):
        fill = fill_ref[r]
        keys.append(tail_tile(r, 0, fill, unfinished_ref, fresh_ref).astype(BF16))
        values.append(tail_tile(r, 1, fill, unfinished_ref, fresh_ref).astype(BF16))
        held = jnp.where(req == r, fill, held)
    keys.append(jnp.zeros((tail // 2, HD), BF16))
    values.append(jnp.zeros((tail // 2, HD), BF16))
    valid = (token // PAGE == req) & (token % PAGE < held + step + 1)
    bias = jnp.where((lane >= PAIRS) | valid, 0.0, NEG).astype(BF16)
    bias = jnp.concatenate([bias_ref[...], bias], 0)
    mixed, log = attend(request_ref[:ROWS, :], jnp.concatenate(keys, 0), jnp.concatenate(values, 0), bias)
    mixed_ref[...] = mixed
    log_ref[...] = log


def local_part(fill, request, pool, unfinished, fresh, bias):
    out = pltpu.VMEM((ROWS, HD), F32)
    request, bias = keep(request, bias)
    return pl.pallas_call(
        local_kernel,
        out_shape=(out, out),
        in_specs=[SMEM] + [VMEM] * 5,
        out_specs=(VMEM, VMEM),
        cost_estimate=pl.CostEstimate(flops=2**28, bytes_accessed=2**20, transcendentals=2**18),
        name="local_part",
    )(fill, request, pool, unfinished, fresh, bias)


def arrived_part(request_ref, bias_ref, tiles_ref, which):
    tiles = tiles_ref[:, 2 * which : 2 * which + 2]
    key = tiles[:, :, :PAGE, :].reshape(TOKENS, HD)
    value = tiles[:, :, PAGE:, :].reshape(TOKENS, HD)
    bias = jnp.where(key > MARK / 2, jnp.asarray(NEG, BF16), bias_ref[...])
    return attend(request_ref[:ROWS, :], key, value, bias)


def far_kernel(request_ref, bias_ref, tiles_ref, after_ref, out_ref):
    mixed, log = arrived_part(request_ref, bias_ref, tiles_ref, 1)
    out_ref[:ROWS, :] = mixed.astype(BF16)
    lane = iota((ROWS, HD), 1)
    high = log.astype(BF16).astype(F32)
    middle = (log - high).astype(BF16).astype(F32)
    least = log - high - middle
    parts = jnp.where(lane == 0, high, jnp.where(lane == 1, middle, jnp.where(lane == 2, least, 0.0)))
    eye = (iota((8, HD), 0) == iota((8, HD), 1)).astype(BF16)
    across = dot(eye, parts.astype(BF16), 1, 1)
    out_ref[ROWS:, :] = jnp.concatenate([across[:, :HD], across[:, HD:]], 0).astype(BF16)


def far_part(request, bias, tiles, after):
    return pl.pallas_call(
        far_kernel,
        out_shape=pltpu.VMEM((ROWS + 16, HD), BF16),
        in_specs=[VMEM] * 3 + [pl.BlockSpec(memory_space=pl.ANY)],
        out_specs=VMEM,
        cost_estimate=pl.CostEstimate(flops=2**28, bytes_accessed=2**20, transcendentals=2**18),
        name="far_part",
    )(*keep(request, bias, tiles, after))


def near_kernel(request_ref, bias_ref, tiles_ref, mixed_ref, log_ref, out_ref, sum_ref):
    part = arrived_part(request_ref, bias_ref, tiles_ref, 0)
    mixed, log = combine((mixed_ref[...], log_ref[...]), part)
    out_ref[...] = mixed
    sum_ref[...] = log


def near_part(request, bias, tiles, mixed, log):
    out = pltpu.VMEM((ROWS, HD), F32)
    return pl.pallas_call(
        near_kernel,
        out_shape=(out, out),
        in_specs=[VMEM] * 5,
        out_specs=(VMEM, VMEM),
        cost_estimate=pl.CostEstimate(flops=2**28, bytes_accessed=2**20, transcendentals=2**18),
        name="near_part",
    )(*keep(request, bias, tiles, mixed, log))


def merge_kernel(mixed_ref, log_ref, back_ref, attn_ref, square_ref):
    stats = back_ref[ROWS:, :].astype(F32)
    stats = jnp.concatenate([stats[:8], stats[8:]], 1).astype(BF16)
    log = dot(stats, jnp.ones((8, HD), BF16), 0, 0)
    mixed, _ = combine((mixed_ref[...], log_ref[...]), (back_ref[:ROWS, :].astype(F32), log))
    attn = mixed.astype(BF16)
    attn_ref[...] = attn
    wide = attn.astype(F32)
    square = wide * wide
    total = square[:PAIRS]
    for h in range(1, HEADS):
        total = total + square[h * PAIRS : (h + 1) * PAIRS]
    total = jnp.sum(total, axis=-1, keepdims=True)
    line = jnp.sum(jnp.where(iota((PAIRS, HD), 0) == iota((PAIRS, HD), 1), total, 0.0), axis=0, keepdims=True)
    square_ref[...] = jnp.broadcast_to(line[None], square_ref.shape)


def merge(mixed, log, back, ways):
    return pl.pallas_call(
        merge_kernel,
        out_shape=(pltpu.VMEM((ROWS, HD), BF16), pltpu.VMEM((ways, 1, HD), F32)),
        in_specs=[VMEM] * 3,
        out_specs=(VMEM, VMEM),
        name="merge",
    )(*keep(mixed, log, back))


def norm_kernel(attn_ref, square_ref, gain_ref, out_ref):
    ways = square_ref.shape[0]
    line = square_ref[0]
    for i in range(1, ways):
        line = line + square_ref[i]
    line = jnp.broadcast_to(line, (PAIRS, HD))
    total = jnp.sum(jnp.where(iota((PAIRS, HD), 0) == iota((PAIRS, HD), 1), line, 0.0), axis=1, keepdims=True)
    scale = lax.rsqrt(total / (ways * HEADS * HD) + 1e-5)
    for h in range(HEADS):
        wide = attn_ref[h * PAIRS : (h + 1) * PAIRS, :].astype(F32)
        out = wide * scale * gain_ref[h : h + 1, :]
        for t in range(STEPS):
            out_ref[t, :, h * HD : (h + 1) * HD] = out[t * REQS : (t + 1) * REQS].astype(BF16)


def normalize(attn, square, gain):
    return pl.pallas_call(
        norm_kernel,
        out_shape=jax.ShapeDtypeStruct((STEPS, REQS, HEADS * HD), BF16),
        in_specs=[VMEM] * 3,
        out_specs=VMEM,
        name="normalize",
    )(*keep(attn, square, gain))


def body(
    lookup_vectors,
    fresh_token_memory,
    unfinished_block_memory,
    cache_block_store,
    sequence_block_index,
    sequence_history_count,
    unfinished_block_fill,
    migration_sender_block,
    migration_receiver_server,
    switch_moment,
    output_scaling_weights,
):
    ways = lax.axis_size("tp")
    half = lax.axis_index("zh").astype(I32).reshape(1)
    pool = cache_block_store.reshape(POOL, 2 * PAGE, HD)
    unfinished = unfinished_block_memory.reshape(REQS, 2 * PAGE, HD)
    fresh = fresh_token_memory.reshape(STEPS, REQS, 2, HD)
    gain = output_scaling_weights.reshape(HEADS, HD)
    fill, switch = unfinished_block_fill, switch_moment

    outgoing = send_tiles(
        half, migration_receiver_server.reshape(MIGS), migration_sender_block, fill, switch, pool, unfinished, fresh
    )
    tiles = lax.all_to_all(outgoing, ("y", "zl", "x"), split_axis=0, concat_axis=0, tiled=True)
    tiles = tiles.reshape(PEERS, 4, 2 * PAGE, HD)

    query = jnp.transpose(lookup_vectors, (2, 0, 1, 3)).reshape(ROWS, HD)
    request = request_rows(sequence_history_count, switch, query, sequence_block_index)
    asked = lax.ppermute(request, "zh", [(0, 1), (1, 0)])
    pool_bias, near_bias = token_bias(("pool", "arrived"), half, request)
    mixed, log = local_part(fill, request, pool, unfinished, fresh, pool_bias)
    (far_bias,) = token_bias(("arrived",), half, asked)

    back = lax.ppermute(far_part(asked, far_bias, tiles, log), "zh", [(0, 1), (1, 0)])
    mixed, log = near_part(request, near_bias, tiles, mixed, log)
    attn, square = merge(mixed, log, back, ways)
    square = lax.all_to_all(square, "tp", split_axis=0, concat_axis=0, tiled=True)
    return normalize(attn, square, gain)


def solution(mesh):
    devices = mesh.devices.reshape(4, 2, 2, 4, mesh.devices.shape[1])
    fine = jax.sharding.Mesh(devices, ("y", "zh", "zl", "x", "tp"))
    rep = ("y", "zh", "zl", "x")
    placed = (
        P(None, rep, "tp", None),
        P(None, rep, None, "tp", None),
        P(rep, None, None, "tp", None),
        P(rep, None, None, "tp", None),
        P(rep, None),
        P(rep),
        P(rep),
        P(rep),
        P(rep, None),
        P(rep),
        P("tp"),
    )
    return jax.shard_map(body, mesh=fine, in_specs=placed, out_specs=P(None, rep, "tp"), check_vma=False)
```

```python
import jax
import jax.numpy as jnp
from jax import lax
from jax.experimental import pallas as pl
from jax.experimental.pallas import tpu as pltpu
from jax.sharding import PartitionSpec as P

STEPS, REQS, HEADS, HD = 4, 4, 16, 128
ROWS = STEPS * REQS * HEADS
PAIRS = STEPS * REQS
PAGE = 16
POOL = 64
MIGS = 64
PEERS = 32
TOKENS = POOL * PAGE
NEG = -1e30
MARK = 4096.0
SCALE = 1.4426950408889634 / HD**0.5
HALVES = [[p for p in reversed(range(64)) if (p >> 3) & 1 == half] for half in range(2)]
PARTNERS = [(p, p ^ 8) for p in range(64)]
SUMMED = [[4, 5, 2, 3, 6, 7, 0, 1]]
F32, BF16, I32 = jnp.float32, jnp.bfloat16, jnp.int32
VMEM = pl.BlockSpec(memory_space=pltpu.VMEM)
SMEM = pl.BlockSpec(memory_space=pltpu.SMEM)


def dot(a, b, ca, cb):
    return lax.dot_general(a, b, (((ca,), (cb,)), ((), ())), preferred_element_type=F32)


def iota(shape, axis):
    return lax.broadcasted_iota(I32, shape, axis)


def tail_tile(r, kv, fill, unfinished_ref, fresh_ref):
    rows = iota((PAGE, HD), 0)
    tile = unfinished_ref[r, kv * PAGE : (kv + 1) * PAGE, :].astype(F32)
    for s in range(STEPS):
        row = fresh_ref[s, r].astype(F32)[kv : kv + 1, :]
        tile = jnp.where(rows == fill + s, row, tile)
    return tile


def send_kernel(half_ref, target_ref, source_ref, fill_ref, switch_ref, pool_ref, unfinished_ref, fresh_ref, out_ref, cut_ref):
    rows = iota((PAGE, HD), 0)
    blank = jnp.concatenate([jnp.full((PAGE, HD), MARK, BF16), jnp.zeros((PAGE, HD), BF16)], 0)
    out_ref[...] = jnp.broadcast_to(blank[None], out_ref.shape)
    for r in range(REQS):
        fill = fill_ref[r]
        key = tail_tile(r, 0, fill, unfinished_ref, fresh_ref)
        value = tail_tile(r, 1, fill, unfinished_ref, fresh_ref)
        key = jnp.where(rows < fill + switch_ref[r], key, MARK)
        cut_ref[r] = jnp.concatenate([key, value], 0).astype(BF16)
    half = half_ref[0]
    low = jnp.int32(0)
    high = jnp.int32(0)
    for e in range(MIGS):
        t = target_ref[e]
        m = source_ref[e]
        first = t < 32
        shift = t & 31
        word = jnp.where(first, low, high)
        rank = (word >> shift) & 1
        word = word | (jnp.int32(1) << shift)
        low = jnp.where(first, word, low)
        high = jnp.where(first, high, word)
        peer = (((t >> 4) << 3) | (t & 7)) ^ (PEERS - 1)
        which = ((t >> 3) & 1) ^ half
        slot = peer * 4 + which * 2 + rank
        pooled = pool_ref[jnp.minimum(m, POOL - 1)]
        cut = cut_ref[jnp.maximum(m - POOL, 0)]
        out_ref[slot] = jnp.where(m < POOL, pooled, cut)


def keep(*arrays):
    return tuple(pltpu.with_memory_space_constraint(x, pltpu.VMEM) for x in arrays)


def send_tiles(half, target, source, fill, switch, pool, unfinished, fresh):
    return pl.pallas_call(
        send_kernel,
        out_shape=pltpu.VMEM((PEERS * 4, 2 * PAGE, HD), BF16),
        in_specs=[SMEM] * 5 + [VMEM] * 3,
        out_specs=VMEM,
        scratch_shapes=[pltpu.VMEM((REQS, 2 * PAGE, HD), BF16)],
        cost_estimate=pl.CostEstimate(flops=1000, bytes_accessed=2**21, transcendentals=0),
        name="send_tiles",
    )(half, target, source, fill, switch, pool, unfinished, fresh)


def request_kernel(length_ref, switch_ref, query_ref, table_ref, out_ref):
    out_ref[:ROWS, :] = query_ref[...]
    row, lane = iota((16, HD), 0), iota((16, HD), 1)
    info = jnp.concatenate([table_ref[...], jnp.zeros((16 - REQS, HD), I32)], 0)
    for g in range(REQS):
        length = length_ref[g]
        at = row - REQS
        fact = jnp.where(at == 0, length >> 4, jnp.where(at == 1, length & 15, switch_ref[g]))
        info = jnp.where((lane == g) & (at >= 0) & (at < 3), fact, info)
    out_ref[ROWS:, :] = info.astype(F32).astype(BF16)


def request_rows(length, switch, query, table):
    return pl.pallas_call(
        request_kernel,
        out_shape=pltpu.VMEM((ROWS + 16, HD), BF16),
        in_specs=[SMEM] * 2 + [VMEM] * 2,
        out_specs=VMEM,
        cost_estimate=pl.CostEstimate(flops=1000, bytes_accessed=2**17, transcendentals=0),
        name="request_rows",
    )(length, switch, query, table)


def bias_kernel(sections, half_ref, request_ref, *refs):
    info = request_ref[ROWS:, :].astype(F32).astype(I32)
    half = half_ref[0]
    token = iota((TOKENS, HD), 0)
    entry = iota((TOKENS, HD), 1)
    place, offset = token // PAGE, token % PAGE
    lane = iota((1, HD), 1)
    pair, part = lane % PAIRS, lane // PAIRS
    step, req = pair // REQS, pair % REQS
    inside, weights = [], []
    late = jnp.zeros((1, HD), jnp.bool_)
    for g in range(REQS):
        pages, rest, moment = (info[REQS + i : REQS + i + 1, g : g + 1] for i in range(3))
        inside.append(entry * PAGE + offset < pages * PAGE + rest)
        late = late | ((req == g) & (step < moment))
        spread = iota((HD, HD), 1)
        weights.append(((spread % REQS == g) & (spread < 3 * PAIRS)).astype(BF16))
    weights = jnp.concatenate(weights, 0)
    for section, ref in zip(sections, refs, strict=True):
        if section == "pool":
            page = place
        else:
            from_end = place ^ (2 * PEERS - 2)
            page = POOL + (from_end // 16) * 32 + half * 16 + from_end % 16
        hits = [jnp.where((info[g : g + 1, :] == page) & inside[g], 1.0, 0.0).astype(BF16) for g in range(REQS)]
        count = dot(jnp.concatenate(hits, 1), weights, 1, 0)
        log = jnp.log2(jnp.maximum(count, 1.0)) / SCALE
        high = log.astype(BF16).astype(F32)
        middle = (log - high).astype(BF16).astype(F32)
        parts = jnp.where(part == 0, high, jnp.where(part == 1, middle, log - high - middle))
        gone = count == 0
        if section != "pool":
            gone = gone | late
        ref[...] = jnp.where(gone, jnp.where(part == 0, NEG, 0.0), parts).astype(BF16)


def token_bias(sections, half, request):
    out = pltpu.VMEM((TOKENS, HD), BF16)
    return pl.pallas_call(
        lambda *refs: bias_kernel(sections, *refs),
        out_shape=(out,) * len(sections),
        in_specs=[SMEM, VMEM],
        out_specs=(VMEM,) * len(sections),
        cost_estimate=pl.CostEstimate(flops=2**27, bytes_accessed=2**18, transcendentals=0),
        name="token_bias",
    )(half, *keep(request))


def attend(query, key, value, bias):
    lane, row = iota((ROWS, HD), 1), iota((ROWS, HD), 0)
    reads = ((lane % PAIRS == row % PAIRS) & (lane < 3 * PAIRS)).astype(BF16)
    scores = dot(jnp.concatenate([query, reads], 1), jnp.concatenate([key, bias], 1), 1, 1)
    top = jnp.max(scores, axis=-1, keepdims=True)
    probs = jnp.exp2((scores - top) * SCALE).astype(BF16)
    mixed = dot(probs, jnp.concatenate([value, jnp.ones(value.shape, BF16)], 1), 1, 0)
    total = mixed[:, HD:]
    return mixed[:, :HD] / total, top * SCALE + jnp.log2(total)


def combine(a, b):
    (x, p), (y, q) = a, b
    top = jnp.maximum(p, q)
    u, v = jnp.exp2(p - top), jnp.exp2(q - top)
    return (x * u + y * v) / (u + v), top + jnp.log2(u + v)


def local_kernel(fill_ref, request_ref, pool_ref, unfinished_ref, fresh_ref, bias_ref, mixed_ref, log_ref):
    tail = 2 * REQS * PAGE
    keys = [pool_ref[:, :PAGE, :].reshape(TOKENS, HD)]
    values = [pool_ref[:, PAGE:, :].reshape(TOKENS, HD)]
    token, lane = iota((tail, HD), 0), iota((tail, HD), 1)
    step, req = lane % PAIRS // REQS, lane % REQS
    held = jnp.zeros((tail, HD), I32)
    for r in range(REQS):
        fill = fill_ref[r]
        keys.append(tail_tile(r, 0, fill, unfinished_ref, fresh_ref).astype(BF16))
        values.append(tail_tile(r, 1, fill, unfinished_ref, fresh_ref).astype(BF16))
        held = jnp.where(req == r, fill, held)
    keys.append(jnp.zeros((tail // 2, HD), BF16))
    values.append(jnp.zeros((tail // 2, HD), BF16))
    valid = (token // PAGE == req) & (token % PAGE < held + step + 1)
    bias = jnp.where((lane >= PAIRS) | valid, 0.0, NEG).astype(BF16)
    bias = jnp.concatenate([bias_ref[...], bias], 0)
    mixed, log = attend(request_ref[:ROWS, :], jnp.concatenate(keys, 0), jnp.concatenate(values, 0), bias)
    mixed_ref[...] = mixed
    log_ref[...] = log


def local_part(fill, request, pool, unfinished, fresh, bias):
    out = pltpu.VMEM((ROWS, HD), F32)
    request, bias = keep(request, bias)
    return pl.pallas_call(
        local_kernel,
        out_shape=(out, out),
        in_specs=[SMEM] + [VMEM] * 5,
        out_specs=(VMEM, VMEM),
        cost_estimate=pl.CostEstimate(flops=2**28, bytes_accessed=2**20, transcendentals=2**18),
        name="local_part",
    )(fill, request, pool, unfinished, fresh, bias)


def arrived_part(request_ref, bias_ref, tiles_ref, which):
    tiles = tiles_ref[:, 2 * which : 2 * which + 2]
    key = tiles[:, :, :PAGE, :].reshape(TOKENS, HD)
    value = tiles[:, :, PAGE:, :].reshape(TOKENS, HD)
    bias = jnp.where(key > MARK / 2, jnp.asarray(NEG, BF16), bias_ref[...])
    return attend(request_ref[:ROWS, :], key, value, bias)


def far_kernel(request_ref, bias_ref, tiles_ref, after_ref, out_ref):
    mixed, log = arrived_part(request_ref, bias_ref, tiles_ref, 1)
    out_ref[:ROWS, :] = mixed.astype(BF16)
    lane = iota((ROWS, HD), 1)
    high = log.astype(BF16).astype(F32)
    middle = (log - high).astype(BF16).astype(F32)
    least = log - high - middle
    parts = jnp.where(lane == 0, high, jnp.where(lane == 1, middle, jnp.where(lane == 2, least, 0.0)))
    eye = (iota((8, HD), 0) == iota((8, HD), 1)).astype(BF16)
    across = dot(eye, parts.astype(BF16), 1, 1)
    out_ref[ROWS:, :] = jnp.concatenate([across[:, :HD], across[:, HD:]], 0).astype(BF16)


def far_part(request, bias, tiles, after):
    return pl.pallas_call(
        far_kernel,
        out_shape=pltpu.VMEM((ROWS + 16, HD), BF16),
        in_specs=[VMEM] * 3 + [pl.BlockSpec(memory_space=pl.ANY)],
        out_specs=VMEM,
        cost_estimate=pl.CostEstimate(flops=2**28, bytes_accessed=2**20, transcendentals=2**18),
        name="far_part",
    )(*keep(request, bias, tiles, after))


def near_kernel(request_ref, bias_ref, tiles_ref, mixed_ref, log_ref, out_ref, sum_ref):
    part = arrived_part(request_ref, bias_ref, tiles_ref, 0)
    mixed, log = combine((mixed_ref[...], log_ref[...]), part)
    out_ref[...] = mixed
    sum_ref[...] = log


def near_part(request, bias, tiles, mixed, log):
    out = pltpu.VMEM((ROWS, HD), F32)
    return pl.pallas_call(
        near_kernel,
        out_shape=(out, out),
        in_specs=[VMEM] * 5,
        out_specs=(VMEM, VMEM),
        cost_estimate=pl.CostEstimate(flops=2**28, bytes_accessed=2**20, transcendentals=2**18),
        name="near_part",
    )(*keep(request, bias, tiles, mixed, log))


def merge_kernel(mixed_ref, log_ref, back_ref, attn_ref, square_ref):
    stats = back_ref[ROWS:, :].astype(F32)
    stats = jnp.concatenate([stats[:8], stats[8:]], 1).astype(BF16)
    log = dot(stats, jnp.ones((8, HD), BF16), 0, 0)
    mixed, _ = combine((mixed_ref[...], log_ref[...]), (back_ref[:ROWS, :].astype(F32), log))
    attn = mixed.astype(BF16)
    attn_ref[...] = attn
    wide = attn.astype(F32)
    square = wide * wide
    total = square[:PAIRS]
    for h in range(1, HEADS):
        total = total + square[h * PAIRS : (h + 1) * PAIRS]
    total = jnp.sum(total, axis=-1, keepdims=True)
    line = jnp.sum(jnp.where(iota((PAIRS, HD), 0) == iota((PAIRS, HD), 1), total, 0.0), axis=0, keepdims=True)
    square_ref[...] = jnp.broadcast_to(line[None], square_ref.shape)


def merge(mixed, log, back, ways):
    return pl.pallas_call(
        merge_kernel,
        out_shape=(pltpu.VMEM((ROWS, HD), BF16), pltpu.VMEM((ways, 1, HD), F32)),
        in_specs=[VMEM] * 3,
        out_specs=(VMEM, VMEM),
        name="merge",
    )(*keep(mixed, log, back))


def norm_kernel(attn_ref, square_ref, gain_ref, out_ref):
    ways = square_ref.shape[0]
    line = square_ref[0]
    for i in range(1, ways):
        line = line + square_ref[i]
    line = jnp.broadcast_to(line, (PAIRS, HD))
    total = jnp.sum(jnp.where(iota((PAIRS, HD), 0) == iota((PAIRS, HD), 1), line, 0.0), axis=1, keepdims=True)
    scale = lax.rsqrt(total / (ways * HEADS * HD) + 1e-5)
    for h in range(HEADS):
        wide = attn_ref[h * PAIRS : (h + 1) * PAIRS, :].astype(F32)
        out = wide * scale * gain_ref[h : h + 1, :]
        for t in range(STEPS):
            out_ref[t, :, h * HD : (h + 1) * HD] = out[t * REQS : (t + 1) * REQS].astype(BF16)


def normalize(attn, square, gain):
    return pl.pallas_call(
        norm_kernel,
        out_shape=jax.ShapeDtypeStruct((STEPS, REQS, HEADS * HD), BF16),
        in_specs=[VMEM] * 3,
        out_specs=VMEM,
        name="normalize",
    )(*keep(attn, square, gain))


def body(
    lookup_vectors,
    fresh_token_memory,
    unfinished_block_memory,
    cache_block_store,
    sequence_block_index,
    sequence_history_count,
    unfinished_block_fill,
    migration_sender_block,
    migration_receiver_server,
    switch_moment,
    output_scaling_weights,
):
    ways = lax.axis_size("tp")
    half = ((lax.axis_index("rep") >> 3) & 1).astype(I32).reshape(1)
    pool = cache_block_store.reshape(POOL, 2 * PAGE, HD)
    unfinished = unfinished_block_memory.reshape(REQS, 2 * PAGE, HD)
    fresh = fresh_token_memory.reshape(STEPS, REQS, 2, HD)
    gain = output_scaling_weights.reshape(HEADS, HD)
    fill, switch = unfinished_block_fill, switch_moment

    outgoing = send_tiles(
        half, migration_receiver_server.reshape(MIGS), migration_sender_block, fill, switch, pool, unfinished, fresh
    )
    tiles = lax.all_to_all(outgoing, "rep", split_axis=0, concat_axis=0, axis_index_groups=HALVES, tiled=True)
    tiles = tiles.reshape(PEERS, 4, 2 * PAGE, HD)

    query = jnp.transpose(lookup_vectors, (2, 0, 1, 3)).reshape(ROWS, HD)
    request = request_rows(sequence_history_count, switch, query, sequence_block_index)
    asked = lax.ppermute(request, "rep", PARTNERS)
    pool_bias, near_bias = token_bias(("pool", "arrived"), half, request)
    mixed, log = local_part(fill, request, pool, unfinished, fresh, pool_bias)
    (far_bias,) = token_bias(("arrived",), half, asked)

    back = lax.ppermute(far_part(asked, far_bias, tiles, log), "rep", PARTNERS)
    mixed, log = near_part(request, near_bias, tiles, mixed, log)
    attn, square = merge(mixed, log, back, ways)
    square = lax.all_to_all(square, "tp", split_axis=0, concat_axis=0, axis_index_groups=SUMMED, tiled=True)
    return normalize(attn, square, gain)


def solution(mesh):
    rep = "rep"
    placed = (
        P(None, rep, "tp", None),
        P(None, rep, None, "tp", None),
        P(rep, None, None, "tp", None),
        P(rep, None, None, "tp", None),
        P(rep, None),
        P(rep),
        P(rep),
        P(rep),
        P(rep, None),
        P(rep),
        P("tp"),
    )
    return jax.shard_map(body, mesh=mesh, in_specs=placed, out_specs=P(None, rep, "tp"), check_vma=False)
```

```python
import jax
import jax.numpy as jnp
from jax import lax
from jax.experimental import pallas as pl
from jax.experimental.pallas import tpu as pltpu
from jax.sharding import PartitionSpec as P

STEPS, REQS, HEADS, HD = 4, 4, 16, 128
ROWS = STEPS * REQS * HEADS
PAIRS = STEPS * REQS
PAGE = 16
POOL = 64
MIGS = 64
PEERS = 32
TOKENS = POOL * PAGE
NEG = -1e30
MARK = 4096.0
SCALE = 1.4426950408889634 / HD**0.5
FIRST = 27
ORDER = [k ^ FIRST for k in range(PEERS)]
HALVES = [[((j >> 3) << 4) | (half << 3) | (j & 7) for j in ORDER] for half in range(2)]
STANDS = [ORDER.index(((t >> 4) << 3) | (t & 7)) * 4 + ((t >> 3) & 1) * 2 for t in range(64)]
PARTNERS = [(p, p ^ 8) for p in range(64)]
SUMMED = [[4, 5, 2, 3, 6, 7, 0, 1]]
F32, BF16, I32 = jnp.float32, jnp.bfloat16, jnp.int32
VMEM = pl.BlockSpec(memory_space=pltpu.VMEM)
SMEM = pl.BlockSpec(memory_space=pltpu.SMEM)


def dot(a, b, ca, cb):
    return lax.dot_general(a, b, (((ca,), (cb,)), ((), ())), preferred_element_type=F32)


def iota(shape, axis):
    return lax.broadcasted_iota(I32, shape, axis)


def tail_tile(r, kv, fill, unfinished_ref, fresh_ref):
    rows = iota((PAGE, HD), 0)
    tile = unfinished_ref[r, kv * PAGE : (kv + 1) * PAGE, :].astype(F32)
    for s in range(STEPS):
        row = fresh_ref[s, r].astype(F32)[kv : kv + 1, :]
        tile = jnp.where(rows == fill + s, row, tile)
    return tile


def send_kernel(
    half_ref, target_ref, source_ref, stand_ref, length_ref, fill_ref, switch_ref,
    pool_ref, unfinished_ref, fresh_ref, query_ref, table_ref, out_ref, request_ref, cut_ref
):
    rows = iota((PAGE, HD), 0)
    blank = jnp.concatenate([jnp.full((PAGE, HD), MARK, BF16), jnp.zeros((PAGE, HD), BF16)], 0)
    out_ref[...] = jnp.broadcast_to(blank[None], out_ref.shape)
    for r in range(REQS):
        fill = fill_ref[r]
        key = tail_tile(r, 0, fill, unfinished_ref, fresh_ref)
        value = tail_tile(r, 1, fill, unfinished_ref, fresh_ref)
        key = jnp.where(rows < fill + switch_ref[r], key, MARK)
        cut_ref[r] = jnp.concatenate([key, value], 0).astype(BF16)
    flip = half_ref[0] * 2
    low = jnp.int32(0)
    high = jnp.int32(0)
    for e in range(MIGS):
        t = target_ref[e]
        m = source_ref[e]
        first = t < 32
        shift = t & 31
        word = jnp.where(first, low, high)
        rank = (word >> shift) & 1
        word = word | (jnp.int32(1) << shift)
        low = jnp.where(first, word, low)
        high = jnp.where(first, high, word)
        pooled = pool_ref[jnp.minimum(m, POOL - 1)]
        cut = cut_ref[jnp.maximum(m - POOL, 0)]
        out_ref[(stand_ref[t] ^ flip) + rank] = jnp.where(m < POOL, pooled, cut)
    query = jnp.transpose(query_ref[...].astype(F32), (1, 0, 2))
    request_ref[:ROWS, :] = query.reshape(ROWS, HD).astype(BF16)
    row, lane = iota((16, HD), 0), iota((16, HD), 1)
    info = jnp.concatenate([table_ref[...], jnp.zeros((16 - REQS, HD), I32)], 0)
    for g in range(REQS):
        length = length_ref[g]
        at = row - REQS
        fact = jnp.where(at == 0, length >> 4, jnp.where(at == 1, length & 15, switch_ref[g]))
        info = jnp.where((lane == g) & (at >= 0) & (at < 3), fact, info)
    request_ref[ROWS:, :] = info.astype(F32).astype(BF16)


def keep(*arrays):
    return tuple(pltpu.with_memory_space_constraint(x, pltpu.VMEM) for x in arrays)


def send_tiles(half, target, source, length, fill, switch, pool, unfinished, fresh, query, table):
    return pl.pallas_call(
        send_kernel,
        out_shape=(pltpu.VMEM((PEERS * 4, 2 * PAGE, HD), BF16), pltpu.VMEM((ROWS + 16, HD), BF16)),
        in_specs=[SMEM] * 7 + [VMEM] * 5,
        out_specs=(VMEM, VMEM),
        scratch_shapes=[pltpu.VMEM((REQS, 2 * PAGE, HD), BF16)],
        cost_estimate=pl.CostEstimate(flops=1000, bytes_accessed=2**21, transcendentals=0),
        name="send_tiles",
    )(half, target, source, jnp.array(STANDS, I32), length, fill, switch, pool, unfinished, fresh, query, table)


def bias_kernel(sections, half_ref, request_ref, *refs):
    info = request_ref[ROWS:, :].astype(F32).astype(I32)
    half = half_ref[0]
    token = iota((TOKENS, HD), 0)
    entry = iota((TOKENS, HD), 1)
    place, offset = token // PAGE, token % PAGE
    lane = iota((1, HD), 1)
    pair, part = lane % PAIRS, lane // PAIRS
    step, req = pair // REQS, pair % REQS
    inside, weights = [], []
    late = jnp.zeros((1, HD), jnp.bool_)
    for g in range(REQS):
        pages, rest, moment = (info[REQS + i : REQS + i + 1, g : g + 1] for i in range(3))
        inside.append(entry * PAGE + offset < pages * PAGE + rest)
        late = late | ((req == g) & (step < moment))
        spread = iota((HD, HD), 1)
        weights.append(((spread % REQS == g) & (spread < 3 * PAIRS)).astype(BF16))
    weights = jnp.concatenate(weights, 0)
    for section, ref in zip(sections, refs, strict=True):
        spot = info[:REQS]
        if section != "pool":
            slot = spot - POOL
            peer = slot >> 1
            here = (slot >= 0) & (((peer >> 3) & 1) == half)
            peer = (((peer >> 4) << 3) | (peer & 7)) ^ FIRST
            spot = jnp.where(here, peer * 2 + (slot & 1), -1)
        hits = [jnp.where((spot[g : g + 1, :] == place) & inside[g], 1.0, 0.0).astype(BF16) for g in range(REQS)]
        count = dot(jnp.concatenate(hits, 1), weights, 1, 0)
        log = jnp.log2(jnp.maximum(count, 1.0)) / SCALE
        high = log.astype(BF16).astype(F32)
        middle = (log - high).astype(BF16).astype(F32)
        parts = jnp.where(part == 0, high, jnp.where(part == 1, middle, log - high - middle))
        gone = count == 0
        if section != "pool":
            gone = gone | late
        ref[...] = jnp.where(gone, jnp.where(part == 0, NEG, 0.0), parts).astype(BF16)


def token_bias(sections, half, request):
    out = pltpu.VMEM((TOKENS, HD), BF16)
    return pl.pallas_call(
        lambda *refs: bias_kernel(sections, *refs),
        out_shape=(out,) * len(sections),
        in_specs=[SMEM, VMEM],
        out_specs=(VMEM,) * len(sections),
        cost_estimate=pl.CostEstimate(flops=2**27, bytes_accessed=2**18, transcendentals=0),
        name="token_bias",
    )(half, *keep(request))


def attend(query, key, value, bias):
    lane, row = iota((ROWS, HD), 1), iota((ROWS, HD), 0)
    reads = ((lane % PAIRS == row % PAIRS) & (lane < 3 * PAIRS)).astype(BF16)
    scores = dot(jnp.concatenate([query, reads], 1), jnp.concatenate([key, bias], 1), 1, 1)
    top = jnp.max(scores, axis=-1, keepdims=True)
    probs = jnp.exp2((scores - top) * SCALE).astype(BF16)
    mixed = dot(probs, jnp.concatenate([value, jnp.ones(value.shape, BF16)], 1), 1, 0)
    total = mixed[:, HD:]
    return mixed[:, :HD] / total, top * SCALE + jnp.log2(total)


def combine(a, b):
    (x, p), (y, q) = a, b
    top = jnp.maximum(p, q)
    u, v = jnp.exp2(p - top), jnp.exp2(q - top)
    return (x * u + y * v) / (u + v), top + jnp.log2(u + v)


def local_kernel(fill_ref, request_ref, pool_ref, unfinished_ref, fresh_ref, bias_ref, mixed_ref, log_ref):
    tail = 2 * REQS * PAGE
    keys = [pool_ref[:, :PAGE, :].reshape(TOKENS, HD)]
    values = [pool_ref[:, PAGE:, :].reshape(TOKENS, HD)]
    token, lane = iota((tail, HD), 0), iota((tail, HD), 1)
    step, req = lane % PAIRS // REQS, lane % REQS
    held = jnp.zeros((tail, HD), I32)
    for r in range(REQS):
        fill = fill_ref[r]
        keys.append(tail_tile(r, 0, fill, unfinished_ref, fresh_ref).astype(BF16))
        values.append(tail_tile(r, 1, fill, unfinished_ref, fresh_ref).astype(BF16))
        held = jnp.where(req == r, fill, held)
    keys.append(jnp.zeros((tail // 2, HD), BF16))
    values.append(jnp.zeros((tail // 2, HD), BF16))
    valid = (token // PAGE == req) & (token % PAGE < held + step + 1)
    bias = jnp.where((lane >= PAIRS) | valid, 0.0, NEG).astype(BF16)
    bias = jnp.concatenate([bias_ref[...], bias], 0)
    mixed, log = attend(request_ref[:ROWS, :], jnp.concatenate(keys, 0), jnp.concatenate(values, 0), bias)
    mixed_ref[...] = mixed
    log_ref[...] = log


def local_part(fill, request, pool, unfinished, fresh, bias):
    out = pltpu.VMEM((ROWS, HD), F32)
    request, bias = keep(request, bias)
    return pl.pallas_call(
        local_kernel,
        out_shape=(out, out),
        in_specs=[SMEM] + [VMEM] * 5,
        out_specs=(VMEM, VMEM),
        cost_estimate=pl.CostEstimate(flops=2**28, bytes_accessed=2**20, transcendentals=2**18),
        name="local_part",
    )(fill, request, pool, unfinished, fresh, bias)


def arrived_part(request_ref, bias_ref, tiles_ref, which):
    tiles = tiles_ref[:, 2 * which : 2 * which + 2]
    key = tiles[:, :, :PAGE, :].reshape(TOKENS, HD)
    value = tiles[:, :, PAGE:, :].reshape(TOKENS, HD)
    bias = jnp.where(key > MARK / 2, jnp.asarray(NEG, BF16), bias_ref[...])
    return attend(request_ref[:ROWS, :], key, value, bias)


def far_kernel(request_ref, bias_ref, tiles_ref, after_ref, out_ref):
    mixed, log = arrived_part(request_ref, bias_ref, tiles_ref, 1)
    out_ref[:ROWS, :] = mixed.astype(BF16)
    lane = iota((ROWS, HD), 1)
    high = log.astype(BF16).astype(F32)
    middle = (log - high).astype(BF16).astype(F32)
    least = log - high - middle
    parts = jnp.where(lane == 0, high, jnp.where(lane == 1, middle, jnp.where(lane == 2, least, 0.0)))
    eye = (iota((8, HD), 0) == iota((8, HD), 1)).astype(BF16)
    across = dot(eye, parts.astype(BF16), 1, 1)
    out_ref[ROWS:, :] = jnp.concatenate([across[:, :HD], across[:, HD:]], 0).astype(BF16)


def far_part(request, bias, tiles, after):
    return pl.pallas_call(
        far_kernel,
        out_shape=pltpu.VMEM((ROWS + 16, HD), BF16),
        in_specs=[VMEM] * 3 + [pl.BlockSpec(memory_space=pl.ANY)],
        out_specs=VMEM,
        cost_estimate=pl.CostEstimate(flops=2**28, bytes_accessed=2**20, transcendentals=2**18),
        name="far_part",
    )(*keep(request, bias, tiles, after))


def near_kernel(request_ref, bias_ref, tiles_ref, mixed_ref, log_ref, out_ref, sum_ref):
    part = arrived_part(request_ref, bias_ref, tiles_ref, 0)
    mixed, log = combine((mixed_ref[...], log_ref[...]), part)
    out_ref[...] = mixed
    sum_ref[...] = log


def near_part(request, bias, tiles, mixed, log):
    out = pltpu.VMEM((ROWS, HD), F32)
    return pl.pallas_call(
        near_kernel,
        out_shape=(out, out),
        in_specs=[VMEM] * 5,
        out_specs=(VMEM, VMEM),
        cost_estimate=pl.CostEstimate(flops=2**28, bytes_accessed=2**20, transcendentals=2**18),
        name="near_part",
    )(*keep(request, bias, tiles, mixed, log))


def merge_kernel(mixed_ref, log_ref, back_ref, attn_ref, square_ref):
    stats = back_ref[ROWS:, :].astype(F32)
    stats = jnp.concatenate([stats[:8], stats[8:]], 1).astype(BF16)
    log = dot(stats, jnp.ones((8, HD), BF16), 0, 0)
    mixed, _ = combine((mixed_ref[...], log_ref[...]), (back_ref[:ROWS, :].astype(F32), log))
    attn = mixed.astype(BF16)
    attn_ref[...] = attn
    wide = attn.astype(F32)
    square = wide * wide
    total = square[:PAIRS]
    for h in range(1, HEADS):
        total = total + square[h * PAIRS : (h + 1) * PAIRS]
    total = jnp.sum(total, axis=-1, keepdims=True)
    line = jnp.sum(jnp.where(iota((PAIRS, HD), 0) == iota((PAIRS, HD), 1), total, 0.0), axis=0, keepdims=True)
    square_ref[...] = jnp.broadcast_to(line[None], square_ref.shape)


def merge(mixed, log, back, ways):
    return pl.pallas_call(
        merge_kernel,
        out_shape=(pltpu.VMEM((ROWS, HD), BF16), pltpu.VMEM((ways, 1, HD), F32)),
        in_specs=[VMEM] * 3,
        out_specs=(VMEM, VMEM),
        name="merge",
    )(*keep(mixed, log, back))


def norm_kernel(attn_ref, square_ref, gain_ref, out_ref):
    ways = square_ref.shape[0]
    line = square_ref[0]
    for i in range(1, ways):
        line = line + square_ref[i]
    line = jnp.broadcast_to(line, (PAIRS, HD))
    total = jnp.sum(jnp.where(iota((PAIRS, HD), 0) == iota((PAIRS, HD), 1), line, 0.0), axis=1, keepdims=True)
    scale = lax.rsqrt(total / (ways * HEADS * HD) + 1e-5)
    for h in range(HEADS):
        wide = attn_ref[h * PAIRS : (h + 1) * PAIRS, :].astype(F32)
        out = wide * scale * gain_ref[h : h + 1, :]
        for t in range(STEPS):
            out_ref[t, :, h * HD : (h + 1) * HD] = out[t * REQS : (t + 1) * REQS].astype(BF16)


def normalize(attn, square, gain):
    return pl.pallas_call(
        norm_kernel,
        out_shape=jax.ShapeDtypeStruct((STEPS, REQS, HEADS * HD), BF16),
        in_specs=[VMEM] * 3,
        out_specs=VMEM,
        name="normalize",
    )(*keep(attn, square, gain))


def body(
    lookup_vectors,
    fresh_token_memory,
    unfinished_block_memory,
    cache_block_store,
    sequence_block_index,
    sequence_history_count,
    unfinished_block_fill,
    migration_sender_block,
    migration_receiver_server,
    switch_moment,
    output_scaling_weights,
):
    ways = lax.axis_size("tp")
    half = ((lax.axis_index("rep") >> 3) & 1).astype(I32).reshape(1)
    pool = cache_block_store.reshape(POOL, 2 * PAGE, HD)
    unfinished = unfinished_block_memory.reshape(REQS, 2 * PAGE, HD)
    fresh = fresh_token_memory.reshape(STEPS, REQS, 2, HD)
    gain = output_scaling_weights.reshape(HEADS, HD)
    fill, switch = unfinished_block_fill, switch_moment

    query = lookup_vectors.reshape(PAIRS, HEADS, HD)
    outgoing, request = send_tiles(
        half, migration_receiver_server.reshape(MIGS), migration_sender_block, sequence_history_count, fill, switch,
        pool, unfinished, fresh, query, sequence_block_index
    )
    tiles = lax.all_to_all(outgoing, "rep", split_axis=0, concat_axis=0, axis_index_groups=HALVES, tiled=True)
    tiles = tiles.reshape(PEERS, 4, 2 * PAGE, HD)

    asked = lax.ppermute(request, "rep", PARTNERS)
    pool_bias, near_bias = token_bias(("pool", "arrived"), half, request)
    mixed, log = local_part(fill, request, pool, unfinished, fresh, pool_bias)
    (far_bias,) = token_bias(("arrived",), half, asked)

    back = lax.ppermute(far_part(asked, far_bias, tiles, log), "rep", PARTNERS)
    mixed, log = near_part(request, near_bias, tiles, mixed, log)
    attn, square = merge(mixed, log, back, ways)
    square = lax.all_to_all(square, "tp", split_axis=0, concat_axis=0, axis_index_groups=SUMMED, tiled=True)
    return normalize(attn, square, gain)


def solution(mesh):
    rep = "rep"
    placed = (
        P(None, rep, "tp", None),
        P(None, rep, None, "tp", None),
        P(rep, None, None, "tp", None),
        P(rep, None, None, "tp", None),
        P(rep, None),
        P(rep),
        P(rep),
        P(rep),
        P(rep, None),
        P(rep),
        P("tp"),
    )
    return jax.shard_map(body, mesh=mesh, in_specs=placed, out_specs=P(None, rep, "tp"), check_vma=False)
```

```python
import jax
import jax.numpy as jnp
from jax import lax
from jax.experimental import pallas as pl
from jax.experimental.pallas import tpu as pltpu
from jax.sharding import PartitionSpec as P

STEPS, REQS, HEADS, HD = 4, 4, 16, 128
ROWS = STEPS * REQS * HEADS
PAIRS = STEPS * REQS
PAGE = 16
POOL = 64
MIGS = 64
PEERS = 32
TOKENS = POOL * PAGE
NEG = -1e30
MARK = 4096.0
SCALE = 1.4426950408889634 / HD**0.5
def place_of(member, core):
    if core == 0:
        return member ^ 27
    place = member ^ 31
    return ((place & 3) << 3) | (place & 4) | (place >> 3)


PLACES = [[place_of(j, core) for j in range(PEERS)] for core in range(2)]
ORDERS = [[places.index(k) for k in range(PEERS)] for places in PLACES]
HALVES = [
    [(((j >> 3) << 4) | (half << 3) | (j & 7)) * 8 + tp for j in ORDERS[tp % 2]] for half in range(2) for tp in range(8)
]
STANDS = [PLACES[c][((t >> 4) << 3) | (t & 7)] * 4 + ((t >> 3) & 1) * 2 for c in range(2) for t in range(64)]
PARTNERS = [(p, p ^ 8) for p in range(64)]
SUMMED = [[4, 5, 2, 3, 6, 7, 0, 1]]
F32, BF16, I32 = jnp.float32, jnp.bfloat16, jnp.int32
VMEM = pl.BlockSpec(memory_space=pltpu.VMEM)
SMEM = pl.BlockSpec(memory_space=pltpu.SMEM)


def dot(a, b, ca, cb):
    return lax.dot_general(a, b, (((ca,), (cb,)), ((), ())), preferred_element_type=F32)


def iota(shape, axis):
    return lax.broadcasted_iota(I32, shape, axis)


def tail_tile(r, kv, fill, unfinished_ref, fresh_ref):
    rows = iota((PAGE, HD), 0)
    tile = unfinished_ref[r, kv * PAGE : (kv + 1) * PAGE, :].astype(F32)
    for s in range(STEPS):
        row = fresh_ref[s, r].astype(F32)[kv : kv + 1, :]
        tile = jnp.where(rows == fill + s, row, tile)
    return tile


def send_kernel(
    half_ref, core_ref, target_ref, source_ref, stand_ref, length_ref, fill_ref, switch_ref,
    pool_ref, unfinished_ref, fresh_ref, query_ref, table_ref, out_ref, request_ref, tiles_ref
):
    rows = iota((PAGE, HD), 0)
    blank = jnp.concatenate([jnp.full((PAGE, HD), MARK, BF16), jnp.zeros((PAGE, HD), BF16)], 0)
    out_ref[...] = jnp.broadcast_to(blank[None], out_ref.shape)
    tiles_ref[:POOL] = pool_ref[...]
    for r in range(REQS):
        fill = fill_ref[r]
        key = tail_tile(r, 0, fill, unfinished_ref, fresh_ref)
        value = tail_tile(r, 1, fill, unfinished_ref, fresh_ref)
        key = jnp.where(rows < fill + switch_ref[r], key, MARK)
        tiles_ref[POOL + r] = jnp.concatenate([key, value], 0).astype(BF16)
    flip = half_ref[0] * 2
    table = core_ref[0] * 64
    low = jnp.int32(0)
    high = jnp.int32(0)
    for e in range(MIGS):
        t = target_ref[e]
        first = t < 32
        shift = t & 31
        word = jnp.where(first, low, high)
        rank = (word >> shift) & 1
        word = word | (jnp.int32(1) << shift)
        low = jnp.where(first, word, low)
        high = jnp.where(first, high, word)
        out_ref[(stand_ref[table + t] ^ flip) + rank] = tiles_ref[source_ref[e]]
    query = jnp.transpose(query_ref[...].astype(F32), (1, 0, 2))
    request_ref[:ROWS, :] = query.reshape(ROWS, HD).astype(BF16)
    row, lane = iota((16, HD), 0), iota((16, HD), 1)
    info = jnp.concatenate([table_ref[...], jnp.zeros((16 - REQS, HD), I32)], 0)
    for g in range(REQS):
        length = length_ref[g]
        at = row - REQS
        fact = jnp.where(at == 0, length >> 4, jnp.where(at == 1, length & 15, switch_ref[g]))
        info = jnp.where((lane == g) & (at >= 0) & (at < 3), fact, info)
    request_ref[ROWS:, :] = info.astype(F32).astype(BF16)


def keep(*arrays):
    return tuple(pltpu.with_memory_space_constraint(x, pltpu.VMEM) for x in arrays)


def send_tiles(half, core, target, source, length, fill, switch, pool, unfinished, fresh, query, table):
    return pl.pallas_call(
        send_kernel,
        out_shape=(pltpu.VMEM((PEERS * 4, 2 * PAGE, HD), BF16), pltpu.VMEM((ROWS + 16, HD), BF16)),
        in_specs=[SMEM] * 8 + [VMEM] * 5,
        out_specs=(VMEM, VMEM),
        scratch_shapes=[pltpu.VMEM((POOL + REQS, 2 * PAGE, HD), BF16)],
        cost_estimate=pl.CostEstimate(flops=1000, bytes_accessed=2**21, transcendentals=0),
        name="send_tiles",
    )(half, core, target, source, jnp.array(STANDS, I32), length, fill, switch, pool, unfinished, fresh, query, table)


def bias_kernel(sections, half_ref, core_ref, request_ref, *refs):
    info = request_ref[ROWS:, :].astype(F32).astype(I32)
    half = half_ref[0]
    token = iota((TOKENS, HD), 0)
    entry = iota((TOKENS, HD), 1)
    place, offset = token // PAGE, token % PAGE
    lane = iota((1, HD), 1)
    pair, part = lane % PAIRS, lane // PAIRS
    step, req = pair // REQS, pair % REQS
    inside, weights = [], []
    late = jnp.zeros((1, HD), jnp.bool_)
    for g in range(REQS):
        pages, rest, moment = (info[REQS + i : REQS + i + 1, g : g + 1] for i in range(3))
        inside.append(entry * PAGE + offset < pages * PAGE + rest)
        late = late | ((req == g) & (step < moment))
        spread = iota((HD, HD), 1)
        weights.append(((spread % REQS == g) & (spread < 3 * PAIRS)).astype(BF16))
    weights = jnp.concatenate(weights, 0)
    for section, ref in zip(sections, refs, strict=True):
        spot = info[:REQS]
        if section != "pool":
            slot = spot - POOL
            peer = slot >> 1
            here = (slot >= 0) & (((peer >> 3) & 1) == half)
            peer = ((peer >> 4) << 3) | (peer & 7)
            peer = jnp.where(core_ref[0] == 1, place_of(peer, 1), place_of(peer, 0))
            spot = jnp.where(here, peer * 2 + (slot & 1), -1)
        hits = [jnp.where((spot[g : g + 1, :] == place) & inside[g], 1.0, 0.0).astype(BF16) for g in range(REQS)]
        count = dot(jnp.concatenate(hits, 1), weights, 1, 0)
        log = jnp.log2(jnp.maximum(count, 1.0)) / SCALE
        high = log.astype(BF16).astype(F32)
        middle = (log - high).astype(BF16).astype(F32)
        parts = jnp.where(part == 0, high, jnp.where(part == 1, middle, log - high - middle))
        gone = count == 0
        if section != "pool":
            gone = gone | late
        ref[...] = jnp.where(gone, jnp.where(part == 0, NEG, 0.0), parts).astype(BF16)


def token_bias(sections, half, core, request):
    out = pltpu.VMEM((TOKENS, HD), BF16)
    return pl.pallas_call(
        lambda *refs: bias_kernel(sections, *refs),
        out_shape=(out,) * len(sections),
        in_specs=[SMEM, SMEM, VMEM],
        out_specs=(VMEM,) * len(sections),
        cost_estimate=pl.CostEstimate(flops=2**27, bytes_accessed=2**18, transcendentals=0),
        name="token_bias",
    )(half, core, *keep(request))


def attend(query, key, value, bias):
    lane, row = iota((ROWS, HD), 1), iota((ROWS, HD), 0)
    reads = ((lane % PAIRS == row % PAIRS) & (lane < 3 * PAIRS)).astype(BF16)
    scores = dot(jnp.concatenate([query, reads], 1), jnp.concatenate([key, bias], 1), 1, 1)
    top = jnp.max(scores, axis=-1, keepdims=True)
    probs = jnp.exp2((scores - top) * SCALE).astype(BF16)
    mixed = dot(probs, jnp.concatenate([value, jnp.ones(value.shape, BF16)], 1), 1, 0)
    total = mixed[:, HD:]
    return mixed[:, :HD] / total, top * SCALE + jnp.log2(total)


def combine(a, b):
    (x, p), (y, q) = a, b
    top = jnp.maximum(p, q)
    u, v = jnp.exp2(p - top), jnp.exp2(q - top)
    return (x * u + y * v) / (u + v), top + jnp.log2(u + v)


def local_kernel(fill_ref, request_ref, pool_ref, unfinished_ref, fresh_ref, bias_ref, mixed_ref, log_ref):
    tail = 2 * REQS * PAGE
    keys = [pool_ref[:, :PAGE, :].reshape(TOKENS, HD)]
    values = [pool_ref[:, PAGE:, :].reshape(TOKENS, HD)]
    token, lane = iota((tail, HD), 0), iota((tail, HD), 1)
    step, req = lane % PAIRS // REQS, lane % REQS
    held = jnp.zeros((tail, HD), I32)
    for r in range(REQS):
        fill = fill_ref[r]
        keys.append(tail_tile(r, 0, fill, unfinished_ref, fresh_ref).astype(BF16))
        values.append(tail_tile(r, 1, fill, unfinished_ref, fresh_ref).astype(BF16))
        held = jnp.where(req == r, fill, held)
    keys.append(jnp.zeros((tail // 2, HD), BF16))
    values.append(jnp.zeros((tail // 2, HD), BF16))
    valid = (token // PAGE == req) & (token % PAGE < held + step + 1)
    bias = jnp.where((lane >= PAIRS) | valid, 0.0, NEG).astype(BF16)
    bias = jnp.concatenate([bias_ref[...], bias], 0)
    mixed, log = attend(request_ref[:ROWS, :], jnp.concatenate(keys, 0), jnp.concatenate(values, 0), bias)
    mixed_ref[...] = mixed
    log_ref[...] = log


def local_part(fill, request, pool, unfinished, fresh, bias):
    out = pltpu.VMEM((ROWS, HD), F32)
    request, bias = keep(request, bias)
    return pl.pallas_call(
        local_kernel,
        out_shape=(out, out),
        in_specs=[SMEM] + [VMEM] * 5,
        out_specs=(VMEM, VMEM),
        cost_estimate=pl.CostEstimate(flops=2**28, bytes_accessed=2**20, transcendentals=2**18),
        name="local_part",
    )(fill, request, pool, unfinished, fresh, bias)


def arrived_part(request_ref, bias_ref, tiles_ref, which):
    tiles = tiles_ref[:, 2 * which : 2 * which + 2]
    key = tiles[:, :, :PAGE, :].reshape(TOKENS, HD)
    value = tiles[:, :, PAGE:, :].reshape(TOKENS, HD)
    bias = jnp.where(key > MARK / 2, jnp.asarray(NEG, BF16), bias_ref[...])
    return attend(request_ref[:ROWS, :], key, value, bias)


def far_kernel(request_ref, bias_ref, tiles_ref, after_ref, out_ref):
    mixed, log = arrived_part(request_ref, bias_ref, tiles_ref, 1)
    out_ref[:ROWS, :] = mixed.astype(BF16)
    lane = iota((ROWS, HD), 1)
    high = log.astype(BF16).astype(F32)
    middle = (log - high).astype(BF16).astype(F32)
    least = log - high - middle
    parts = jnp.where(lane == 0, high, jnp.where(lane == 1, middle, jnp.where(lane == 2, least, 0.0)))
    eye = (iota((8, HD), 0) == iota((8, HD), 1)).astype(BF16)
    across = dot(eye, parts.astype(BF16), 1, 1)
    out_ref[ROWS:, :] = jnp.concatenate([across[:, :HD], across[:, HD:]], 0).astype(BF16)


def far_part(request, bias, tiles, after):
    return pl.pallas_call(
        far_kernel,
        out_shape=pltpu.VMEM((ROWS + 16, HD), BF16),
        in_specs=[VMEM] * 3 + [pl.BlockSpec(memory_space=pl.ANY)],
        out_specs=VMEM,
        cost_estimate=pl.CostEstimate(flops=2**28, bytes_accessed=2**20, transcendentals=2**18),
        name="far_part",
    )(*keep(request, bias, tiles, after))


def near_kernel(request_ref, bias_ref, tiles_ref, mixed_ref, log_ref, out_ref, sum_ref):
    part = arrived_part(request_ref, bias_ref, tiles_ref, 0)
    mixed, log = combine((mixed_ref[...], log_ref[...]), part)
    out_ref[...] = mixed
    sum_ref[...] = log


def near_part(request, bias, tiles, mixed, log):
    out = pltpu.VMEM((ROWS, HD), F32)
    return pl.pallas_call(
        near_kernel,
        out_shape=(out, out),
        in_specs=[VMEM] * 5,
        out_specs=(VMEM, VMEM),
        cost_estimate=pl.CostEstimate(flops=2**28, bytes_accessed=2**20, transcendentals=2**18),
        name="near_part",
    )(*keep(request, bias, tiles, mixed, log))


def merge_kernel(mixed_ref, log_ref, back_ref, attn_ref, square_ref):
    stats = back_ref[ROWS:, :].astype(F32)
    stats = jnp.concatenate([stats[:8], stats[8:]], 1).astype(BF16)
    log = dot(stats, jnp.ones((8, HD), BF16), 0, 0)
    mixed, _ = combine((mixed_ref[...], log_ref[...]), (back_ref[:ROWS, :].astype(F32), log))
    attn = mixed.astype(BF16)
    attn_ref[...] = attn
    wide = attn.astype(F32)
    square = wide * wide
    total = square[:PAIRS]
    for h in range(1, HEADS):
        total = total + square[h * PAIRS : (h + 1) * PAIRS]
    total = jnp.sum(total, axis=-1, keepdims=True)
    line = jnp.sum(jnp.where(iota((PAIRS, HD), 0) == iota((PAIRS, HD), 1), total, 0.0), axis=0, keepdims=True)
    square_ref[...] = jnp.broadcast_to(line[None], square_ref.shape)


def merge(mixed, log, back, ways):
    return pl.pallas_call(
        merge_kernel,
        out_shape=(pltpu.VMEM((ROWS, HD), BF16), pltpu.VMEM((ways, 1, HD), F32)),
        in_specs=[VMEM] * 3,
        out_specs=(VMEM, VMEM),
        name="merge",
    )(*keep(mixed, log, back))


def norm_kernel(attn_ref, square_ref, gain_ref, out_ref):
    ways = square_ref.shape[0]
    line = square_ref[0]
    for i in range(1, ways):
        line = line + square_ref[i]
    line = jnp.broadcast_to(line, (PAIRS, HD))
    total = jnp.sum(jnp.where(iota((PAIRS, HD), 0) == iota((PAIRS, HD), 1), line, 0.0), axis=1, keepdims=True)
    scale = lax.rsqrt(total / (ways * HEADS * HD) + 1e-5)
    for h in range(HEADS):
        wide = attn_ref[h * PAIRS : (h + 1) * PAIRS, :].astype(F32)
        out = wide * scale * gain_ref[h : h + 1, :]
        for t in range(STEPS):
            out_ref[t, :, h * HD : (h + 1) * HD] = out[t * REQS : (t + 1) * REQS].astype(BF16)


def normalize(attn, square, gain):
    return pl.pallas_call(
        norm_kernel,
        out_shape=jax.ShapeDtypeStruct((STEPS, REQS, HEADS * HD), BF16),
        in_specs=[VMEM] * 3,
        out_specs=VMEM,
        name="normalize",
    )(*keep(attn, square, gain))


def body(
    lookup_vectors,
    fresh_token_memory,
    unfinished_block_memory,
    cache_block_store,
    sequence_block_index,
    sequence_history_count,
    unfinished_block_fill,
    migration_sender_block,
    migration_receiver_server,
    switch_moment,
    output_scaling_weights,
):
    ways = lax.axis_size("tp")
    half = ((lax.axis_index("rep") >> 3) & 1).astype(I32).reshape(1)
    core = (lax.axis_index("tp") & 1).astype(I32).reshape(1)
    pool = cache_block_store.reshape(POOL, 2 * PAGE, HD)
    unfinished = unfinished_block_memory.reshape(REQS, 2 * PAGE, HD)
    fresh = fresh_token_memory.reshape(STEPS, REQS, 2, HD)
    gain = output_scaling_weights.reshape(HEADS, HD)
    fill, switch = unfinished_block_fill, switch_moment

    query = lookup_vectors.reshape(PAIRS, HEADS, HD)
    outgoing, request = send_tiles(
        half, core, migration_receiver_server.reshape(MIGS), migration_sender_block, sequence_history_count, fill, switch,
        pool, unfinished, fresh, query, sequence_block_index
    )
    tiles = lax.all_to_all(outgoing, ("rep", "tp"), split_axis=0, concat_axis=0, axis_index_groups=HALVES, tiled=True)
    tiles = tiles.reshape(PEERS, 4, 2 * PAGE, HD)

    asked = lax.ppermute(request, "rep", PARTNERS)
    pool_bias, near_bias = token_bias(("pool", "arrived"), half, core, request)
    mixed, log = local_part(fill, request, pool, unfinished, fresh, pool_bias)
    (far_bias,) = token_bias(("arrived",), half, core, asked)

    back = lax.ppermute(far_part(asked, far_bias, tiles, log), "rep", PARTNERS)
    mixed, log = near_part(request, near_bias, tiles, mixed, log)
    attn, square = merge(mixed, log, back, ways)
    square = lax.all_to_all(square, "tp", split_axis=0, concat_axis=0, axis_index_groups=SUMMED, tiled=True)
    return normalize(attn, square, gain)


def solution(mesh):
    rep = "rep"
    placed = (
        P(None, rep, "tp", None),
        P(None, rep, None, "tp", None),
        P(rep, None, None, "tp", None),
        P(rep, None, None, "tp", None),
        P(rep, None),
        P(rep),
        P(rep),
        P(rep),
        P(rep, None),
        P(rep),
        P("tp"),
    )
    return jax.shard_map(body, mesh=mesh, in_specs=placed, out_specs=P(None, rep, "tp"), check_vma=False)
```

```python
import jax
import jax.numpy as jnp
from jax import lax
from jax.experimental import pallas as pl
from jax.experimental.pallas import tpu as pltpu
from jax.sharding import PartitionSpec as P

STEPS, REQS, HEADS, HD = 4, 4, 16, 128
ROWS = STEPS * REQS * HEADS
PAIRS = STEPS * REQS
PAGE = 16
POOL = 64
MIGS = 64
PEERS = 32
TOKENS = POOL * PAGE
NEG = -1e30
MARK = 4096.0
SCALE = 1.4426950408889634 / HD**0.5
def place_of(member, core):
    if core == 0:
        return member ^ 27
    place = member ^ 31
    return ((place & 3) << 3) | (place & 4) | (place >> 3)


PLACES = [[place_of(j, core) for j in range(PEERS)] for core in range(2)]
ORDERS = [[places.index(k) for k in range(PEERS)] for places in PLACES]


def half_of(replica, core):
    half = (replica >> 3) & 1
    return half if core else half ^ ((replica >> 2) & 1)


def replica_of(member, half, core):
    zh = half if core else half ^ ((member >> 2) & 1)
    return ((member >> 3) << 4) | (zh << 3) | (member & 7)


def stand_of(target, core):
    far = half_of(target, core)
    image = target if core or not far else target ^ 4
    return PLACES[core][((image >> 4) << 3) | (image & 7)] * 4 + far * 2


HALVES = [[replica_of(j, half, tp % 2) * 8 + tp for j in ORDERS[tp % 2]] for half in range(2) for tp in range(8)]
STANDS = [stand_of(t, c) for c in range(2) for t in range(64)]
PARTNERS = [(p * 8 + tp, (p ^ (8 if tp % 2 else 4)) * 8 + tp) for p in range(64) for tp in range(8)]
SUMMED = [[4, 5, 2, 3, 6, 7, 0, 1]]
F32, BF16, I32 = jnp.float32, jnp.bfloat16, jnp.int32
VMEM = pl.BlockSpec(memory_space=pltpu.VMEM)
SMEM = pl.BlockSpec(memory_space=pltpu.SMEM)


def dot(a, b, ca, cb):
    return lax.dot_general(a, b, (((ca,), (cb,)), ((), ())), preferred_element_type=F32)


def iota(shape, axis):
    return lax.broadcasted_iota(I32, shape, axis)


def tail_tile(r, kv, fill, unfinished_ref, fresh_ref):
    rows = iota((PAGE, HD), 0)
    tile = unfinished_ref[r, kv * PAGE : (kv + 1) * PAGE, :].astype(F32)
    for s in range(STEPS):
        row = fresh_ref[s, r].astype(F32)[kv : kv + 1, :]
        tile = jnp.where(rows == fill + s, row, tile)
    return tile


def send_kernel(
    half_ref, core_ref, target_ref, source_ref, stand_ref, length_ref, fill_ref, switch_ref,
    pool_ref, unfinished_ref, fresh_ref, query_ref, table_ref, out_ref, request_ref, tiles_ref
):
    rows = iota((PAGE, HD), 0)
    blank = jnp.concatenate([jnp.full((PAGE, HD), MARK, BF16), jnp.zeros((PAGE, HD), BF16)], 0)
    out_ref[...] = jnp.broadcast_to(blank[None], out_ref.shape)
    tiles_ref[:POOL] = pool_ref[...]
    for r in range(REQS):
        fill = fill_ref[r]
        key = tail_tile(r, 0, fill, unfinished_ref, fresh_ref)
        value = tail_tile(r, 1, fill, unfinished_ref, fresh_ref)
        key = jnp.where(rows < fill + switch_ref[r], key, MARK)
        tiles_ref[POOL + r] = jnp.concatenate([key, value], 0).astype(BF16)
    flip = half_ref[0] * jnp.where(core_ref[0] == 1, 2, 2 + 4 * 4)
    table = core_ref[0] * 64
    low = jnp.int32(0)
    high = jnp.int32(0)
    for e in range(MIGS):
        t = target_ref[e]
        first = t < 32
        shift = t & 31
        word = jnp.where(first, low, high)
        rank = (word >> shift) & 1
        word = word | (jnp.int32(1) << shift)
        low = jnp.where(first, word, low)
        high = jnp.where(first, high, word)
        out_ref[(stand_ref[table + t] ^ flip) + rank] = tiles_ref[source_ref[e]]
    query = jnp.transpose(query_ref[...].astype(F32), (1, 0, 2))
    request_ref[:ROWS, :] = query.reshape(ROWS, HD).astype(BF16)
    row, lane = iota((16, HD), 0), iota((16, HD), 1)
    info = jnp.concatenate([table_ref[...], jnp.zeros((16 - REQS, HD), I32)], 0)
    for g in range(REQS):
        length = length_ref[g]
        at = row - REQS
        fact = jnp.where(at == 0, length >> 4, jnp.where(at == 1, length & 15, switch_ref[g]))
        info = jnp.where((lane == g) & (at >= 0) & (at < 3), fact, info)
    request_ref[ROWS:, :] = info.astype(F32).astype(BF16)


def keep(*arrays):
    return tuple(pltpu.with_memory_space_constraint(x, pltpu.VMEM) for x in arrays)


def send_tiles(half, core, target, source, length, fill, switch, pool, unfinished, fresh, query, table):
    return pl.pallas_call(
        send_kernel,
        out_shape=(pltpu.VMEM((PEERS * 4, 2 * PAGE, HD), BF16), pltpu.VMEM((ROWS + 16, HD), BF16)),
        in_specs=[SMEM] * 8 + [VMEM] * 5,
        out_specs=(VMEM, VMEM),
        scratch_shapes=[pltpu.VMEM((POOL + REQS, 2 * PAGE, HD), BF16)],
        cost_estimate=pl.CostEstimate(flops=1000, bytes_accessed=2**21, transcendentals=0),
        name="send_tiles",
    )(half, core, target, source, jnp.array(STANDS, I32), length, fill, switch, pool, unfinished, fresh, query, table)


def bias_kernel(sections, half_ref, core_ref, request_ref, *refs):
    info = request_ref[ROWS:, :].astype(F32).astype(I32)
    half = half_ref[0]
    token = iota((TOKENS, HD), 0)
    entry = iota((1, HD), 1)
    lane = iota((1, HD), 1)
    pair, part = lane % PAIRS, lane // PAIRS
    step, req = pair // REQS, pair % REQS
    held, weights = [], []
    late = jnp.zeros((1, HD), jnp.bool_)
    for g in range(REQS):
        pages, rest, moment = (info[REQS + i : REQS + i + 1, g : g + 1] for i in range(3))
        held.append(jnp.clip(pages * PAGE + rest - entry * PAGE, 0, PAGE).astype(jnp.uint32))
        late = late | ((req == g) & (step < moment))
        spread = iota((HD, HD), 1)
        weights.append(((spread % REQS == g) & (spread < 3 * PAIRS)).astype(BF16))
    weights = jnp.concatenate(weights, 0)
    for section, ref in zip(sections, refs, strict=True):
        spot = info[:REQS]
        if section != "pool":
            slot = spot - POOL
            peer = slot >> 1
            side = jnp.where(core_ref[0] == 1, half_of(peer, 1), half_of(peer, 0))
            here = (slot >= 0) & (side == half)
            peer = ((peer >> 4) << 3) | (peer & 7)
            peer = jnp.where(core_ref[0] == 1, place_of(peer, 1), place_of(peer, 0))
            spot = jnp.where(here, peer * 2 + (slot & 1), POOL)
        first = spot * PAGE
        hits = [
            jnp.where((token - first[g : g + 1, :]).astype(jnp.uint32) < held[g], 1.0, 0.0).astype(BF16) for g in range(REQS)
        ]
        count = dot(jnp.concatenate(hits, 1), weights, 1, 0)
        log = jnp.log2(jnp.maximum(count, 1.0)) * (1.0 / SCALE)
        high = log.astype(BF16).astype(F32)
        middle = (log - high).astype(BF16).astype(F32)
        parts = jnp.where(part == 0, high, jnp.where(part == 1, middle, log - high - middle))
        gone = count == 0
        if section != "pool":
            gone = gone | late
        ref[...] = jnp.where(gone, jnp.where(part == 0, NEG, 0.0), parts).astype(BF16)


def token_bias(sections, half, core, request):
    out = pltpu.VMEM((TOKENS, HD), BF16)
    return pl.pallas_call(
        lambda *refs: bias_kernel(sections, *refs),
        out_shape=(out,) * len(sections),
        in_specs=[SMEM, SMEM, VMEM],
        out_specs=(VMEM,) * len(sections),
        cost_estimate=pl.CostEstimate(flops=2**27, bytes_accessed=2**18, transcendentals=0),
        name="token_bias",
    )(half, core, *keep(request))


def attend(query, key, value, bias):
    lane, row = iota((ROWS, HD), 1), iota((ROWS, HD), 0)
    reads = ((lane % PAIRS == row % PAIRS) & (lane < 3 * PAIRS)).astype(BF16)
    scores = dot(jnp.concatenate([query, reads], 1), jnp.concatenate([key, bias], 1), 1, 1)
    top = jnp.max(scores, axis=-1, keepdims=True)
    probs = jnp.exp2((scores - top) * SCALE).astype(BF16)
    mixed = dot(probs, jnp.concatenate([value, jnp.ones(value.shape, BF16)], 1), 1, 0)
    total = mixed[:, HD:]
    return mixed[:, :HD] / total, top * SCALE + jnp.log2(total)


def combine(a, b):
    (x, p), (y, q) = a, b
    top = jnp.maximum(p, q)
    u, v = jnp.exp2(p - top), jnp.exp2(q - top)
    return (x * u + y * v) / (u + v), top + jnp.log2(u + v)


def local_kernel(fill_ref, request_ref, pool_ref, unfinished_ref, fresh_ref, bias_ref, mixed_ref, log_ref):
    tail = 2 * REQS * PAGE
    keys = [pool_ref[:, :PAGE, :].reshape(TOKENS, HD)]
    values = [pool_ref[:, PAGE:, :].reshape(TOKENS, HD)]
    token, lane = iota((tail, HD), 0), iota((tail, HD), 1)
    step, req = lane % PAIRS // REQS, lane % REQS
    held = jnp.zeros((tail, HD), I32)
    for r in range(REQS):
        fill = fill_ref[r]
        keys.append(tail_tile(r, 0, fill, unfinished_ref, fresh_ref).astype(BF16))
        values.append(tail_tile(r, 1, fill, unfinished_ref, fresh_ref).astype(BF16))
        held = jnp.where(req == r, fill, held)
    keys.append(jnp.zeros((tail // 2, HD), BF16))
    values.append(jnp.zeros((tail // 2, HD), BF16))
    valid = (token // PAGE == req) & (token % PAGE < held + step + 1)
    bias = jnp.where((lane >= PAIRS) | valid, 0.0, NEG).astype(BF16)
    bias = jnp.concatenate([bias_ref[...], bias], 0)
    mixed, log = attend(request_ref[:ROWS, :], jnp.concatenate(keys, 0), jnp.concatenate(values, 0), bias)
    mixed_ref[...] = mixed
    log_ref[...] = log


def local_part(fill, request, pool, unfinished, fresh, bias):
    out = pltpu.VMEM((ROWS, HD), F32)
    request, bias = keep(request, bias)
    return pl.pallas_call(
        local_kernel,
        out_shape=(out, out),
        in_specs=[SMEM] + [VMEM] * 5,
        out_specs=(VMEM, VMEM),
        cost_estimate=pl.CostEstimate(flops=2**28, bytes_accessed=2**20, transcendentals=2**18),
        name="local_part",
    )(fill, request, pool, unfinished, fresh, bias)


def arrived_part(request_ref, bias_ref, tiles_ref, which):
    tiles = tiles_ref[:, 2 * which : 2 * which + 2]
    key = tiles[:, :, :PAGE, :].reshape(TOKENS, HD)
    value = tiles[:, :, PAGE:, :].reshape(TOKENS, HD)
    bias = jnp.where(key > MARK / 2, jnp.asarray(NEG, BF16), bias_ref[...])
    return attend(request_ref[:ROWS, :], key, value, bias)


def far_kernel(request_ref, bias_ref, tiles_ref, after_ref, out_ref):
    mixed, log = arrived_part(request_ref, bias_ref, tiles_ref, 1)
    out_ref[:ROWS, :] = mixed.astype(BF16)
    lane = iota((ROWS, HD), 1)
    high = log.astype(BF16).astype(F32)
    middle = (log - high).astype(BF16).astype(F32)
    least = log - high - middle
    parts = jnp.where(lane == 0, high, jnp.where(lane == 1, middle, jnp.where(lane == 2, least, 0.0)))
    eye = (iota((8, HD), 0) == iota((8, HD), 1)).astype(BF16)
    across = dot(eye, parts.astype(BF16), 1, 1)
    out_ref[ROWS:, :] = jnp.concatenate([across[:, :HD], across[:, HD:]], 0).astype(BF16)


def far_part(request, bias, tiles, after):
    return pl.pallas_call(
        far_kernel,
        out_shape=pltpu.VMEM((ROWS + 16, HD), BF16),
        in_specs=[VMEM] * 3 + [pl.BlockSpec(memory_space=pl.ANY)],
        out_specs=VMEM,
        cost_estimate=pl.CostEstimate(flops=2**28, bytes_accessed=2**20, transcendentals=2**18),
        name="far_part",
    )(*keep(request, bias, tiles, after))


def near_kernel(request_ref, bias_ref, tiles_ref, mixed_ref, log_ref, out_ref, sum_ref):
    part = arrived_part(request_ref, bias_ref, tiles_ref, 0)
    mixed, log = combine((mixed_ref[...], log_ref[...]), part)
    out_ref[...] = mixed
    sum_ref[...] = log


def near_part(request, bias, tiles, mixed, log):
    out = pltpu.VMEM((ROWS, HD), F32)
    return pl.pallas_call(
        near_kernel,
        out_shape=(out, out),
        in_specs=[VMEM] * 5,
        out_specs=(VMEM, VMEM),
        cost_estimate=pl.CostEstimate(flops=2**28, bytes_accessed=2**20, transcendentals=2**18),
        name="near_part",
    )(*keep(request, bias, tiles, mixed, log))


def merge_kernel(mixed_ref, log_ref, back_ref, attn_ref, square_ref):
    stats = back_ref[ROWS:, :].astype(F32)
    stats = jnp.concatenate([stats[:8], stats[8:]], 1).astype(BF16)
    log = dot(stats, jnp.ones((8, HD), BF16), 0, 0)
    mixed, _ = combine((mixed_ref[...], log_ref[...]), (back_ref[:ROWS, :].astype(F32), log))
    attn = mixed.astype(BF16)
    attn_ref[...] = attn
    wide = attn.astype(F32)
    square = wide * wide
    total = square[:PAIRS]
    for h in range(1, HEADS):
        total = total + square[h * PAIRS : (h + 1) * PAIRS]
    total = jnp.sum(total, axis=-1, keepdims=True)
    line = jnp.sum(jnp.where(iota((PAIRS, HD), 0) == iota((PAIRS, HD), 1), total, 0.0), axis=0, keepdims=True)
    square_ref[...] = jnp.broadcast_to(line[None], square_ref.shape)


def merge(mixed, log, back, ways):
    return pl.pallas_call(
        merge_kernel,
        out_shape=(pltpu.VMEM((ROWS, HD), BF16), pltpu.VMEM((ways, 1, HD), F32)),
        in_specs=[VMEM] * 3,
        out_specs=(VMEM, VMEM),
        name="merge",
    )(*keep(mixed, log, back))


def norm_kernel(attn_ref, square_ref, gain_ref, out_ref):
    ways = square_ref.shape[0]
    line = square_ref[0]
    for i in range(1, ways):
        line = line + square_ref[i]
    line = jnp.broadcast_to(line, (PAIRS, HD))
    total = jnp.sum(jnp.where(iota((PAIRS, HD), 0) == iota((PAIRS, HD), 1), line, 0.0), axis=1, keepdims=True)
    scale = lax.rsqrt(total / (ways * HEADS * HD) + 1e-5)
    for h in range(HEADS):
        wide = attn_ref[h * PAIRS : (h + 1) * PAIRS, :].astype(F32)
        out = wide * scale * gain_ref[h : h + 1, :]
        for t in range(STEPS):
            out_ref[t, :, h * HD : (h + 1) * HD] = out[t * REQS : (t + 1) * REQS].astype(BF16)


def normalize(attn, square, gain):
    return pl.pallas_call(
        norm_kernel,
        out_shape=jax.ShapeDtypeStruct((STEPS, REQS, HEADS * HD), BF16),
        in_specs=[VMEM] * 3,
        out_specs=VMEM,
        name="normalize",
    )(*keep(attn, square, gain))


def body(
    lookup_vectors,
    fresh_token_memory,
    unfinished_block_memory,
    cache_block_store,
    sequence_block_index,
    sequence_history_count,
    unfinished_block_fill,
    migration_sender_block,
    migration_receiver_server,
    switch_moment,
    output_scaling_weights,
):
    ways = lax.axis_size("tp")
    core = (lax.axis_index("tp") & 1).astype(I32)
    replica = lax.axis_index("rep").astype(I32)
    half = (((replica >> 3) ^ ((replica >> 2) & (1 - core))) & 1).reshape(1)
    core = core.reshape(1)
    pool = cache_block_store.reshape(POOL, 2 * PAGE, HD)
    unfinished = unfinished_block_memory.reshape(REQS, 2 * PAGE, HD)
    fresh = fresh_token_memory.reshape(STEPS, REQS, 2, HD)
    gain = output_scaling_weights.reshape(HEADS, HD)
    fill, switch = unfinished_block_fill, switch_moment

    query = lookup_vectors.reshape(PAIRS, HEADS, HD)
    outgoing, request = send_tiles(
        half, core, migration_receiver_server.reshape(MIGS), migration_sender_block, sequence_history_count, fill, switch,
        pool, unfinished, fresh, query, sequence_block_index
    )
    tiles = lax.all_to_all(outgoing, ("rep", "tp"), split_axis=0, concat_axis=0, axis_index_groups=HALVES, tiled=True)
    tiles = tiles.reshape(PEERS, 4, 2 * PAGE, HD)

    asked = lax.ppermute(request, ("rep", "tp"), PARTNERS)
    pool_bias, near_bias = token_bias(("pool", "arrived"), half, core, request)
    mixed, log = local_part(fill, request, pool, unfinished, fresh, pool_bias)
    (far_bias,) = token_bias(("arrived",), half, core, asked)

    back = lax.ppermute(far_part(asked, far_bias, tiles, log), ("rep", "tp"), PARTNERS)
    mixed, log = near_part(request, near_bias, tiles, mixed, log)
    attn, square = merge(mixed, log, back, ways)
    square = lax.all_to_all(square, "tp", split_axis=0, concat_axis=0, axis_index_groups=SUMMED, tiled=True)
    return normalize(attn, square, gain)


def solution(mesh):
    rep = "rep"
    placed = (
        P(None, rep, "tp", None),
        P(None, rep, None, "tp", None),
        P(rep, None, None, "tp", None),
        P(rep, None, None, "tp", None),
        P(rep, None),
        P(rep),
        P(rep),
        P(rep),
        P(rep, None),
        P(rep),
        P("tp"),
    )
    return jax.shard_map(body, mesh=mesh, in_specs=placed, out_specs=P(None, rep, "tp"), check_vma=False)
```

```python
import jax
import jax.numpy as jnp
from jax import lax
from jax.experimental import pallas as pl
from jax.experimental.pallas import tpu as pltpu
from jax.sharding import PartitionSpec as P

STEPS, REQS, HEADS, HD = 4, 4, 16, 128
ROWS = STEPS * REQS * HEADS
PAIRS = STEPS * REQS
PAGE = 16
POOL = 64
MIGS = 64
PEERS = 32
TOKENS = POOL * PAGE
NEG = -1e30
MARK = 4096.0
SCALE = 1.4426950408889634 / HD**0.5
def place_of(member, core):
    if core == 0:
        return member ^ 18
    place = member ^ 31
    return ((place & 3) << 3) | (place & 4) | (place >> 3)


PLACES = [[place_of(j, core) for j in range(PEERS)] for core in range(2)]
ORDERS = [[places.index(k) for k in range(PEERS)] for places in PLACES]


def half_of(replica, core):
    half = (replica >> 3) & 1
    return half if core else half ^ ((replica >> 2) & 1)


def replica_of(member, half, core):
    zh = half if core else half ^ ((member >> 2) & 1)
    return ((member >> 3) << 4) | (zh << 3) | (member & 7)


def stand_of(target, core):
    far = half_of(target, core)
    image = target if core or not far else target ^ 4
    return PLACES[core][((image >> 4) << 3) | (image & 7)] * 4 + far * 2


HALVES = [[replica_of(j, half, tp % 2) * 8 + tp for j in ORDERS[tp % 2]] for half in range(2) for tp in range(8)]
STANDS = [stand_of(t, c) for c in range(2) for t in range(64)]
PARTNERS = [(p * 8 + tp, (p ^ (8 if tp % 2 else 4)) * 8 + tp) for p in range(64) for tp in range(8)]
SUMMED = [[4, 5, 2, 3, 6, 7, 0, 1]]
F32, BF16, I32 = jnp.float32, jnp.bfloat16, jnp.int32
VMEM = pl.BlockSpec(memory_space=pltpu.VMEM)
SMEM = pl.BlockSpec(memory_space=pltpu.SMEM)


def dot(a, b, ca, cb):
    return lax.dot_general(a, b, (((ca,), (cb,)), ((), ())), preferred_element_type=F32)


def iota(shape, axis):
    return lax.broadcasted_iota(I32, shape, axis)


def tail_tile(r, kv, fill, unfinished_ref, fresh_ref):
    rows = iota((PAGE, HD), 0)
    tile = unfinished_ref[r, kv * PAGE : (kv + 1) * PAGE, :].astype(F32)
    for s in range(STEPS):
        row = fresh_ref[s, r].astype(F32)[kv : kv + 1, :]
        tile = jnp.where(rows == fill + s, row, tile)
    return tile


def send_kernel(
    half_ref, core_ref, target_ref, source_ref, stand_ref, length_ref, fill_ref, switch_ref,
    pool_ref, unfinished_ref, fresh_ref, query_ref, table_ref, out_ref, request_ref, tiles_ref
):
    rows = iota((PAGE, HD), 0)
    blank = jnp.concatenate([jnp.full((PAGE, HD), MARK, BF16), jnp.zeros((PAGE, HD), BF16)], 0)
    out_ref[...] = jnp.broadcast_to(blank[None], out_ref.shape)
    tiles_ref[:POOL] = pool_ref[...]
    for r in range(REQS):
        fill = fill_ref[r]
        key = tail_tile(r, 0, fill, unfinished_ref, fresh_ref)
        value = tail_tile(r, 1, fill, unfinished_ref, fresh_ref)
        key = jnp.where(rows < fill + switch_ref[r], key, MARK)
        tiles_ref[POOL + r] = jnp.concatenate([key, value], 0).astype(BF16)
    flip = half_ref[0] * jnp.where(core_ref[0] == 1, 2, 2 + 4 * 4)
    table = core_ref[0] * 64
    low = jnp.int32(0)
    high = jnp.int32(0)
    for e in range(MIGS):
        t = target_ref[e]
        first = t < 32
        shift = t & 31
        word = jnp.where(first, low, high)
        rank = (word >> shift) & 1
        word = word | (jnp.int32(1) << shift)
        low = jnp.where(first, word, low)
        high = jnp.where(first, high, word)
        out_ref[(stand_ref[table + t] ^ flip) + rank] = tiles_ref[source_ref[e]]
    query = jnp.transpose(query_ref[...].astype(F32), (1, 0, 2))
    request_ref[:ROWS, :] = query.reshape(ROWS, HD).astype(BF16)
    row, lane = iota((16, HD), 0), iota((16, HD), 1)
    info = jnp.concatenate([table_ref[...], jnp.zeros((16 - REQS, HD), I32)], 0)
    for g in range(REQS):
        length = length_ref[g]
        at = row - REQS
        fact = jnp.where(at == 0, length >> 4, jnp.where(at == 1, length & 15, switch_ref[g]))
        info = jnp.where((lane == g) & (at >= 0) & (at < 3), fact, info)
    request_ref[ROWS:, :] = info.astype(F32).astype(BF16)


def keep(*arrays):
    return tuple(pltpu.with_memory_space_constraint(x, pltpu.VMEM) for x in arrays)


def send_tiles(half, core, target, source, length, fill, switch, pool, unfinished, fresh, query, table):
    return pl.pallas_call(
        send_kernel,
        out_shape=(pltpu.VMEM((PEERS * 4, 2 * PAGE, HD), BF16), pltpu.VMEM((ROWS + 16, HD), BF16)),
        in_specs=[SMEM] * 8 + [VMEM] * 5,
        out_specs=(VMEM, VMEM),
        scratch_shapes=[pltpu.VMEM((POOL + REQS, 2 * PAGE, HD), BF16)],
        cost_estimate=pl.CostEstimate(flops=1000, bytes_accessed=2**21, transcendentals=0),
        name="send_tiles",
    )(half, core, target, source, jnp.array(STANDS, I32), length, fill, switch, pool, unfinished, fresh, query, table)


def bias_kernel(sections, half_ref, core_ref, request_ref, *refs):
    info = request_ref[ROWS:, :].astype(F32).astype(I32)
    half = half_ref[0]
    token = iota((TOKENS, HD), 0)
    entry = iota((1, HD), 1)
    lane = iota((1, HD), 1)
    pair, part = lane % PAIRS, lane // PAIRS
    step, req = pair // REQS, pair % REQS
    held, weights = [], []
    late = jnp.zeros((1, HD), jnp.bool_)
    for g in range(REQS):
        pages, rest, moment = (info[REQS + i : REQS + i + 1, g : g + 1] for i in range(3))
        held.append(jnp.clip(pages * PAGE + rest - entry * PAGE, 0, PAGE).astype(jnp.uint32))
        late = late | ((req == g) & (step < moment))
        spread = iota((HD, HD), 1)
        weights.append(((spread % REQS == g) & (spread < 3 * PAIRS)).astype(BF16))
    weights = jnp.concatenate(weights, 0)
    for section, ref in zip(sections, refs, strict=True):
        spot = info[:REQS]
        if section != "pool":
            slot = spot - POOL
            peer = slot >> 1
            side = jnp.where(core_ref[0] == 1, half_of(peer, 1), half_of(peer, 0))
            here = (slot >= 0) & (side == half)
            peer = ((peer >> 4) << 3) | (peer & 7)
            peer = jnp.where(core_ref[0] == 1, place_of(peer, 1), place_of(peer, 0))
            spot = jnp.where(here, peer * 2 + (slot & 1), POOL)
        first = spot * PAGE
        hits = [
            jnp.where((token - first[g : g + 1, :]).astype(jnp.uint32) < held[g], 1.0, 0.0).astype(BF16) for g in range(REQS)
        ]
        count = dot(jnp.concatenate(hits, 1), weights, 1, 0)
        log = jnp.log2(jnp.maximum(count, 1.0)) * (1.0 / SCALE)
        high = log.astype(BF16).astype(F32)
        middle = (log - high).astype(BF16).astype(F32)
        parts = jnp.where(part == 0, high, jnp.where(part == 1, middle, log - high - middle))
        gone = count == 0
        if section != "pool":
            gone = gone | late
        ref[...] = jnp.where(gone, jnp.where(part == 0, NEG, 0.0), parts).astype(BF16)


def token_bias(sections, half, core, request):
    out = pltpu.VMEM((TOKENS, HD), BF16)
    return pl.pallas_call(
        lambda *refs: bias_kernel(sections, *refs),
        out_shape=(out,) * len(sections),
        in_specs=[SMEM, SMEM, VMEM],
        out_specs=(VMEM,) * len(sections),
        cost_estimate=pl.CostEstimate(flops=2**27, bytes_accessed=2**18, transcendentals=0),
        name="token_bias",
    )(half, core, *keep(request))


def attend(query, key, value, bias):
    lane, row = iota((ROWS, HD), 1), iota((ROWS, HD), 0)
    reads = ((lane % PAIRS == row % PAIRS) & (lane < 3 * PAIRS)).astype(BF16)
    scores = dot(jnp.concatenate([query, reads], 1), jnp.concatenate([key, bias], 1), 1, 1)
    top = jnp.max(scores, axis=-1, keepdims=True)
    probs = jnp.exp2((scores - top) * SCALE).astype(BF16)
    mixed = dot(probs, jnp.concatenate([value, jnp.ones(value.shape, BF16)], 1), 1, 0)
    total = mixed[:, HD:]
    return mixed[:, :HD] / total, top * SCALE + jnp.log2(total)


def combine(a, b):
    (x, p), (y, q) = a, b
    top = jnp.maximum(p, q)
    u, v = jnp.exp2(p - top), jnp.exp2(q - top)
    return (x * u + y * v) / (u + v), top + jnp.log2(u + v)


def local_kernel(fill_ref, request_ref, pool_ref, unfinished_ref, fresh_ref, bias_ref, mixed_ref, log_ref):
    tail = 2 * REQS * PAGE
    keys = [pool_ref[:, :PAGE, :].reshape(TOKENS, HD)]
    values = [pool_ref[:, PAGE:, :].reshape(TOKENS, HD)]
    token, lane = iota((tail, HD), 0), iota((tail, HD), 1)
    step, req = lane % PAIRS // REQS, lane % REQS
    held = jnp.zeros((tail, HD), I32)
    for r in range(REQS):
        fill = fill_ref[r]
        keys.append(tail_tile(r, 0, fill, unfinished_ref, fresh_ref).astype(BF16))
        values.append(tail_tile(r, 1, fill, unfinished_ref, fresh_ref).astype(BF16))
        held = jnp.where(req == r, fill, held)
    keys.append(jnp.zeros((tail // 2, HD), BF16))
    values.append(jnp.zeros((tail // 2, HD), BF16))
    valid = (token // PAGE == req) & (token % PAGE < held + step + 1)
    bias = jnp.where((lane >= PAIRS) | valid, 0.0, NEG).astype(BF16)
    bias = jnp.concatenate([bias_ref[...], bias], 0)
    mixed, log = attend(request_ref[:ROWS, :], jnp.concatenate(keys, 0), jnp.concatenate(values, 0), bias)
    mixed_ref[...] = mixed
    log_ref[...] = log


def local_part(fill, request, pool, unfinished, fresh, bias):
    out = pltpu.VMEM((ROWS, HD), F32)
    request, bias = keep(request, bias)
    return pl.pallas_call(
        local_kernel,
        out_shape=(out, out),
        in_specs=[SMEM] + [VMEM] * 5,
        out_specs=(VMEM, VMEM),
        cost_estimate=pl.CostEstimate(flops=2**28, bytes_accessed=2**20, transcendentals=2**18),
        name="local_part",
    )(fill, request, pool, unfinished, fresh, bias)


def arrived_part(request_ref, bias_ref, tiles_ref, which):
    tiles = tiles_ref[:, 2 * which : 2 * which + 2]
    key = tiles[:, :, :PAGE, :].reshape(TOKENS, HD)
    value = tiles[:, :, PAGE:, :].reshape(TOKENS, HD)
    bias = jnp.where(key > MARK / 2, jnp.asarray(NEG, BF16), bias_ref[...])
    return attend(request_ref[:ROWS, :], key, value, bias)


def far_kernel(request_ref, bias_ref, tiles_ref, after_ref, out_ref):
    mixed, log = arrived_part(request_ref, bias_ref, tiles_ref, 1)
    out_ref[:ROWS, :] = mixed.astype(BF16)
    lane = iota((ROWS, HD), 1)
    high = log.astype(BF16).astype(F32)
    middle = (log - high).astype(BF16).astype(F32)
    least = log - high - middle
    parts = jnp.where(lane == 0, high, jnp.where(lane == 1, middle, jnp.where(lane == 2, least, 0.0)))
    eye = (iota((8, HD), 0) == iota((8, HD), 1)).astype(BF16)
    across = dot(eye, parts.astype(BF16), 1, 1)
    out_ref[ROWS:, :] = jnp.concatenate([across[:, :HD], across[:, HD:]], 0).astype(BF16)


def far_part(request, bias, tiles, after):
    return pl.pallas_call(
        far_kernel,
        out_shape=pltpu.VMEM((ROWS + 16, HD), BF16),
        in_specs=[VMEM] * 3 + [pl.BlockSpec(memory_space=pl.ANY)],
        out_specs=VMEM,
        cost_estimate=pl.CostEstimate(flops=2**28, bytes_accessed=2**20, transcendentals=2**18),
        name="far_part",
    )(*keep(request, bias, tiles, after))


def near_kernel(request_ref, bias_ref, tiles_ref, mixed_ref, log_ref, out_ref, sum_ref):
    part = arrived_part(request_ref, bias_ref, tiles_ref, 0)
    mixed, log = combine((mixed_ref[...], log_ref[...]), part)
    out_ref[...] = mixed
    sum_ref[...] = log


def near_part(request, bias, tiles, mixed, log):
    out = pltpu.VMEM((ROWS, HD), F32)
    return pl.pallas_call(
        near_kernel,
        out_shape=(out, out),
        in_specs=[VMEM] * 5,
        out_specs=(VMEM, VMEM),
        cost_estimate=pl.CostEstimate(flops=2**28, bytes_accessed=2**20, transcendentals=2**18),
        name="near_part",
    )(*keep(request, bias, tiles, mixed, log))


def merge_kernel(mixed_ref, log_ref, back_ref, attn_ref, square_ref):
    stats = back_ref[ROWS:, :].astype(F32)
    stats = jnp.concatenate([stats[:8], stats[8:]], 1).astype(BF16)
    log = dot(stats, jnp.ones((8, HD), BF16), 0, 0)
    mixed, _ = combine((mixed_ref[...], log_ref[...]), (back_ref[:ROWS, :].astype(F32), log))
    attn = mixed.astype(BF16)
    attn_ref[...] = attn
    wide = attn.astype(F32)
    square = wide * wide
    total = square[:PAIRS]
    for h in range(1, HEADS):
        total = total + square[h * PAIRS : (h + 1) * PAIRS]
    total = jnp.sum(total, axis=-1, keepdims=True)
    line = jnp.sum(jnp.where(iota((PAIRS, HD), 0) == iota((PAIRS, HD), 1), total, 0.0), axis=0, keepdims=True)
    square_ref[...] = jnp.broadcast_to(line[None], square_ref.shape)


def merge(mixed, log, back, ways):
    return pl.pallas_call(
        merge_kernel,
        out_shape=(pltpu.VMEM((ROWS, HD), BF16), pltpu.VMEM((ways, 1, HD), F32)),
        in_specs=[VMEM] * 3,
        out_specs=(VMEM, VMEM),
        name="merge",
    )(*keep(mixed, log, back))


def norm_kernel(attn_ref, square_ref, gain_ref, out_ref):
    ways = square_ref.shape[0]
    line = square_ref[0]
    for i in range(1, ways):
        line = line + square_ref[i]
    line = jnp.broadcast_to(line, (PAIRS, HD))
    total = jnp.sum(jnp.where(iota((PAIRS, HD), 0) == iota((PAIRS, HD), 1), line, 0.0), axis=1, keepdims=True)
    scale = lax.rsqrt(total / (ways * HEADS * HD) + 1e-5)
    for h in range(HEADS):
        wide = attn_ref[h * PAIRS : (h + 1) * PAIRS, :].astype(F32)
        out = wide * scale * gain_ref[h : h + 1, :]
        for t in range(STEPS):
            out_ref[t, :, h * HD : (h + 1) * HD] = out[t * REQS : (t + 1) * REQS].astype(BF16)


def normalize(attn, square, gain):
    return pl.pallas_call(
        norm_kernel,
        out_shape=jax.ShapeDtypeStruct((STEPS, REQS, HEADS * HD), BF16),
        in_specs=[VMEM] * 3,
        out_specs=VMEM,
        name="normalize",
    )(*keep(attn, square, gain))


def body(
    lookup_vectors,
    fresh_token_memory,
    unfinished_block_memory,
    cache_block_store,
    sequence_block_index,
    sequence_history_count,
    unfinished_block_fill,
    migration_sender_block,
    migration_receiver_server,
    switch_moment,
    output_scaling_weights,
):
    ways = lax.axis_size("tp")
    core = (lax.axis_index("tp") & 1).astype(I32)
    replica = lax.axis_index("rep").astype(I32)
    half = (((replica >> 3) ^ ((replica >> 2) & (1 - core))) & 1).reshape(1)
    core = core.reshape(1)
    pool = cache_block_store.reshape(POOL, 2 * PAGE, HD)
    unfinished = unfinished_block_memory.reshape(REQS, 2 * PAGE, HD)
    fresh = fresh_token_memory.reshape(STEPS, REQS, 2, HD)
    gain = output_scaling_weights.reshape(HEADS, HD)
    fill, switch = unfinished_block_fill, switch_moment

    query = lookup_vectors.reshape(PAIRS, HEADS, HD)
    outgoing, request = send_tiles(
        half, core, migration_receiver_server.reshape(MIGS), migration_sender_block, sequence_history_count, fill, switch,
        pool, unfinished, fresh, query, sequence_block_index
    )
    tiles = lax.all_to_all(outgoing, ("rep", "tp"), split_axis=0, concat_axis=0, axis_index_groups=HALVES, tiled=True)
    tiles = tiles.reshape(PEERS, 4, 2 * PAGE, HD)

    asked = lax.ppermute(request, ("rep", "tp"), PARTNERS)
    pool_bias, near_bias = token_bias(("pool", "arrived"), half, core, request)
    mixed, log = local_part(fill, request, pool, unfinished, fresh, pool_bias)
    (far_bias,) = token_bias(("arrived",), half, core, asked)

    back = lax.ppermute(far_part(asked, far_bias, tiles, log), ("rep", "tp"), PARTNERS)
    mixed, log = near_part(request, near_bias, tiles, mixed, log)
    attn, square = merge(mixed, log, back, ways)
    square = lax.all_to_all(square, "tp", split_axis=0, concat_axis=0, axis_index_groups=SUMMED, tiled=True)
    return normalize(attn, square, gain)


def solution(mesh):
    rep = "rep"
    placed = (
        P(None, rep, "tp", None),
        P(None, rep, None, "tp", None),
        P(rep, None, None, "tp", None),
        P(rep, None, None, "tp", None),
        P(rep, None),
        P(rep),
        P(rep),
        P(rep),
        P(rep, None),
        P(rep),
        P("tp"),
    )
    return jax.shard_map(body, mesh=mesh, in_specs=placed, out_specs=P(None, rep, "tp"), check_vma=False)
```

```python
import jax
import jax.numpy as jnp
from jax import lax
from jax.experimental import pallas as pl
from jax.experimental.pallas import tpu as pltpu
from jax.sharding import PartitionSpec as P

STEPS, REQS, HEADS, HD = 4, 4, 16, 128
ROWS = STEPS * REQS * HEADS
PAIRS = STEPS * REQS
PAGE = 16
POOL = 64
MIGS = 64
PEERS = 32
TOKENS = POOL * PAGE
NEG = -1e30
MARK = 4096.0
SCALE = 1.4426950408889634 / HD**0.5
def place_of(member, core):
    if core == 0:
        return member ^ 18
    place = member ^ 18
    return ((place & 3) << 3) | (place & 4) | (place >> 3)


PLACES = [[place_of(j, core) for j in range(PEERS)] for core in range(2)]
ORDERS = [[places.index(k) for k in range(PEERS)] for places in PLACES]


def half_of(replica, core):
    half = (replica >> 3) & 1
    return half if core else half ^ ((replica >> 2) & 1)


def replica_of(member, half, core):
    zh = half if core else half ^ ((member >> 2) & 1)
    return ((member >> 3) << 4) | (zh << 3) | (member & 7)


def stand_of(target, core):
    far = half_of(target, core)
    image = target if core or not far else target ^ 4
    return PLACES[core][((image >> 4) << 3) | (image & 7)] * 4 + far * 2


HALVES = [[replica_of(j, half, tp % 2) * 8 + tp for j in ORDERS[tp % 2]] for half in range(2) for tp in range(8)]
STANDS = [stand_of(t, c) for c in range(2) for t in range(64)]
PARTNERS = [(p * 8 + tp, (p ^ (8 if tp % 2 else 4)) * 8 + tp) for p in range(64) for tp in range(8)]
SUMMED = [[4, 5, 2, 3, 6, 7, 0, 1]]
F32, BF16, I32 = jnp.float32, jnp.bfloat16, jnp.int32
VMEM = pl.BlockSpec(memory_space=pltpu.VMEM)
SMEM = pl.BlockSpec(memory_space=pltpu.SMEM)


def dot(a, b, ca, cb):
    return lax.dot_general(a, b, (((ca,), (cb,)), ((), ())), preferred_element_type=F32)


def iota(shape, axis):
    return lax.broadcasted_iota(I32, shape, axis)


def tail_tile(r, kv, fill, unfinished_ref, fresh_ref):
    rows = iota((PAGE, HD), 0)
    tile = unfinished_ref[r, kv * PAGE : (kv + 1) * PAGE, :].astype(F32)
    for s in range(STEPS):
        row = fresh_ref[s, r].astype(F32)[kv : kv + 1, :]
        tile = jnp.where(rows == fill + s, row, tile)
    return tile


def send_kernel(
    half_ref, core_ref, target_ref, source_ref, stand_ref, length_ref, fill_ref, switch_ref,
    pool_ref, unfinished_ref, fresh_ref, query_ref, table_ref, out_ref, request_ref, tiles_ref
):
    rows = iota((PAGE, HD), 0)
    blank = jnp.concatenate([jnp.full((PAGE, HD), MARK, BF16), jnp.zeros((PAGE, HD), BF16)], 0)
    out_ref[...] = jnp.broadcast_to(blank[None], out_ref.shape)
    tiles_ref[:POOL] = pool_ref[...]
    for r in range(REQS):
        fill = fill_ref[r]
        key = tail_tile(r, 0, fill, unfinished_ref, fresh_ref)
        value = tail_tile(r, 1, fill, unfinished_ref, fresh_ref)
        key = jnp.where(rows < fill + switch_ref[r], key, MARK)
        tiles_ref[POOL + r] = jnp.concatenate([key, value], 0).astype(BF16)
    flip = half_ref[0] * jnp.where(core_ref[0] == 1, 2, 2 + 4 * 4)
    table = core_ref[0] * 64
    low = jnp.int32(0)
    high = jnp.int32(0)
    for e in range(MIGS):
        t = target_ref[e]
        first = t < 32
        shift = t & 31
        word = jnp.where(first, low, high)
        rank = (word >> shift) & 1
        word = word | (jnp.int32(1) << shift)
        low = jnp.where(first, word, low)
        high = jnp.where(first, high, word)
        out_ref[(stand_ref[table + t] ^ flip) + rank] = tiles_ref[source_ref[e]]
    query = jnp.transpose(query_ref[...].astype(F32), (1, 0, 2))
    request_ref[:ROWS, :] = query.reshape(ROWS, HD).astype(BF16)
    row, lane = iota((16, HD), 0), iota((16, HD), 1)
    info = jnp.concatenate([table_ref[...], jnp.zeros((16 - REQS, HD), I32)], 0)
    for g in range(REQS):
        length = length_ref[g]
        at = row - REQS
        fact = jnp.where(at == 0, length >> 4, jnp.where(at == 1, length & 15, switch_ref[g]))
        info = jnp.where((lane == g) & (at >= 0) & (at < 3), fact, info)
    request_ref[ROWS:, :] = info.astype(F32).astype(BF16)


def keep(*arrays):
    return tuple(pltpu.with_memory_space_constraint(x, pltpu.VMEM) for x in arrays)


def send_tiles(half, core, target, source, length, fill, switch, pool, unfinished, fresh, query, table):
    return pl.pallas_call(
        send_kernel,
        out_shape=(pltpu.VMEM((PEERS * 4, 2 * PAGE, HD), BF16), pltpu.VMEM((ROWS + 16, HD), BF16)),
        in_specs=[SMEM] * 8 + [VMEM] * 5,
        out_specs=(VMEM, VMEM),
        scratch_shapes=[pltpu.VMEM((POOL + REQS, 2 * PAGE, HD), BF16)],
        cost_estimate=pl.CostEstimate(flops=1000, bytes_accessed=2**21, transcendentals=0),
        name="send_tiles",
    )(half, core, target, source, jnp.array(STANDS, I32), length, fill, switch, pool, unfinished, fresh, query, table)


def bias_kernel(sections, half_ref, core_ref, request_ref, *refs):
    info = request_ref[ROWS:, :].astype(F32).astype(I32)
    half = half_ref[0]
    token = iota((TOKENS, HD), 0)
    entry = iota((1, HD), 1)
    lane = iota((1, HD), 1)
    pair, part = lane % PAIRS, lane // PAIRS
    step, req = pair // REQS, pair % REQS
    held, weights = [], []
    late = jnp.zeros((1, HD), jnp.bool_)
    for g in range(REQS):
        pages, rest, moment = (info[REQS + i : REQS + i + 1, g : g + 1] for i in range(3))
        held.append(jnp.clip(pages * PAGE + rest - entry * PAGE, 0, PAGE).astype(jnp.uint32))
        late = late | ((req == g) & (step < moment))
        spread = iota((HD, HD), 1)
        weights.append(((spread % REQS == g) & (spread < 3 * PAIRS)).astype(BF16))
    weights = jnp.concatenate(weights, 0)
    for section, ref in zip(sections, refs, strict=True):
        spot = info[:REQS]
        if section != "pool":
            slot = spot - POOL
            peer = slot >> 1
            side = jnp.where(core_ref[0] == 1, half_of(peer, 1), half_of(peer, 0))
            here = (slot >= 0) & (side == half)
            peer = ((peer >> 4) << 3) | (peer & 7)
            peer = jnp.where(core_ref[0] == 1, place_of(peer, 1), place_of(peer, 0))
            spot = jnp.where(here, peer * 2 + (slot & 1), POOL)
        first = spot * PAGE
        hits = [
            jnp.where((token - first[g : g + 1, :]).astype(jnp.uint32) < held[g], 1.0, 0.0).astype(BF16) for g in range(REQS)
        ]
        count = dot(jnp.concatenate(hits, 1), weights, 1, 0)
        log = jnp.log2(jnp.maximum(count, 1.0)) * (1.0 / SCALE)
        high = log.astype(BF16).astype(F32)
        middle = (log - high).astype(BF16).astype(F32)
        parts = jnp.where(part == 0, high, jnp.where(part == 1, middle, log - high - middle))
        gone = count == 0
        if section != "pool":
            gone = gone | late
        ref[...] = jnp.where(gone, jnp.where(part == 0, NEG, 0.0), parts).astype(BF16)


def token_bias(sections, half, core, request):
    out = pltpu.VMEM((TOKENS, HD), BF16)
    return pl.pallas_call(
        lambda *refs: bias_kernel(sections, *refs),
        out_shape=(out,) * len(sections),
        in_specs=[SMEM, SMEM, VMEM],
        out_specs=(VMEM,) * len(sections),
        cost_estimate=pl.CostEstimate(flops=2**27, bytes_accessed=2**18, transcendentals=0),
        name="token_bias",
    )(half, core, *keep(request))


def attend(query, key, value, bias):
    lane, row = iota((ROWS, HD), 1), iota((ROWS, HD), 0)
    reads = ((lane % PAIRS == row % PAIRS) & (lane < 3 * PAIRS)).astype(BF16)
    scores = dot(jnp.concatenate([query, reads], 1), jnp.concatenate([key, bias], 1), 1, 1)
    top = jnp.max(scores, axis=-1, keepdims=True)
    probs = jnp.exp2((scores - top) * SCALE).astype(BF16)
    mixed = dot(probs, jnp.concatenate([value, jnp.ones(value.shape, BF16)], 1), 1, 0)
    total = mixed[:, HD:]
    return mixed[:, :HD] / total, top * SCALE + jnp.log2(total)


def combine(a, b):
    (x, p), (y, q) = a, b
    top = jnp.maximum(p, q)
    u, v = jnp.exp2(p - top), jnp.exp2(q - top)
    return (x * u + y * v) / (u + v), top + jnp.log2(u + v)


def local_kernel(fill_ref, request_ref, pool_ref, unfinished_ref, fresh_ref, bias_ref, mixed_ref, log_ref):
    tail = 2 * REQS * PAGE
    keys = [pool_ref[:, :PAGE, :].reshape(TOKENS, HD)]
    values = [pool_ref[:, PAGE:, :].reshape(TOKENS, HD)]
    token, lane = iota((tail, HD), 0), iota((tail, HD), 1)
    step, req = lane % PAIRS // REQS, lane % REQS
    held = jnp.zeros((tail, HD), I32)
    for r in range(REQS):
        fill = fill_ref[r]
        keys.append(tail_tile(r, 0, fill, unfinished_ref, fresh_ref).astype(BF16))
        values.append(tail_tile(r, 1, fill, unfinished_ref, fresh_ref).astype(BF16))
        held = jnp.where(req == r, fill, held)
    keys.append(jnp.zeros((tail // 2, HD), BF16))
    values.append(jnp.zeros((tail // 2, HD), BF16))
    valid = (token // PAGE == req) & (token % PAGE < held + step + 1)
    bias = jnp.where((lane >= PAIRS) | valid, 0.0, NEG).astype(BF16)
    bias = jnp.concatenate([bias_ref[...], bias], 0)
    mixed, log = attend(request_ref[:ROWS, :], jnp.concatenate(keys, 0), jnp.concatenate(values, 0), bias)
    mixed_ref[...] = mixed
    log_ref[...] = log


def local_part(fill, request, pool, unfinished, fresh, bias):
    out = pltpu.VMEM((ROWS, HD), F32)
    request, bias = keep(request, bias)
    return pl.pallas_call(
        local_kernel,
        out_shape=(out, out),
        in_specs=[SMEM] + [VMEM] * 5,
        out_specs=(VMEM, VMEM),
        cost_estimate=pl.CostEstimate(flops=2**28, bytes_accessed=2**20, transcendentals=2**18),
        name="local_part",
    )(fill, request, pool, unfinished, fresh, bias)


def arrived_part(request_ref, bias_ref, tiles_ref, which):
    tiles = tiles_ref[:, 2 * which : 2 * which + 2]
    key = tiles[:, :, :PAGE, :].reshape(TOKENS, HD)
    value = tiles[:, :, PAGE:, :].reshape(TOKENS, HD)
    bias = jnp.where(key > MARK / 2, jnp.asarray(NEG, BF16), bias_ref[...])
    return attend(request_ref[:ROWS, :], key, value, bias)


def far_kernel(request_ref, bias_ref, tiles_ref, after_ref, out_ref):
    mixed, log = arrived_part(request_ref, bias_ref, tiles_ref, 1)
    out_ref[:ROWS, :] = mixed.astype(BF16)
    lane = iota((ROWS, HD), 1)
    high = log.astype(BF16).astype(F32)
    middle = (log - high).astype(BF16).astype(F32)
    least = log - high - middle
    parts = jnp.where(lane == 0, high, jnp.where(lane == 1, middle, jnp.where(lane == 2, least, 0.0)))
    eye = (iota((8, HD), 0) == iota((8, HD), 1)).astype(BF16)
    across = dot(eye, parts.astype(BF16), 1, 1)
    out_ref[ROWS:, :] = jnp.concatenate([across[:, :HD], across[:, HD:]], 0).astype(BF16)


def far_part(request, bias, tiles, after):
    return pl.pallas_call(
        far_kernel,
        out_shape=pltpu.VMEM((ROWS + 16, HD), BF16),
        in_specs=[VMEM] * 3 + [pl.BlockSpec(memory_space=pl.ANY)],
        out_specs=VMEM,
        cost_estimate=pl.CostEstimate(flops=2**28, bytes_accessed=2**20, transcendentals=2**18),
        name="far_part",
    )(*keep(request, bias, tiles, after))


def near_kernel(request_ref, bias_ref, tiles_ref, mixed_ref, log_ref, out_ref, sum_ref):
    part = arrived_part(request_ref, bias_ref, tiles_ref, 0)
    mixed, log = combine((mixed_ref[...], log_ref[...]), part)
    out_ref[...] = mixed
    sum_ref[...] = log


def near_part(request, bias, tiles, mixed, log):
    out = pltpu.VMEM((ROWS, HD), F32)
    return pl.pallas_call(
        near_kernel,
        out_shape=(out, out),
        in_specs=[VMEM] * 5,
        out_specs=(VMEM, VMEM),
        cost_estimate=pl.CostEstimate(flops=2**28, bytes_accessed=2**20, transcendentals=2**18),
        name="near_part",
    )(*keep(request, bias, tiles, mixed, log))


def merge_kernel(mixed_ref, log_ref, back_ref, attn_ref, square_ref):
    stats = back_ref[ROWS:, :].astype(F32)
    stats = jnp.concatenate([stats[:8], stats[8:]], 1).astype(BF16)
    log = dot(stats, jnp.ones((8, HD), BF16), 0, 0)
    mixed, _ = combine((mixed_ref[...], log_ref[...]), (back_ref[:ROWS, :].astype(F32), log))
    attn = mixed.astype(BF16)
    attn_ref[...] = attn
    wide = attn.astype(F32)
    square = wide * wide
    total = square[:PAIRS]
    for h in range(1, HEADS):
        total = total + square[h * PAIRS : (h + 1) * PAIRS]
    total = jnp.sum(total, axis=-1, keepdims=True)
    line = jnp.sum(jnp.where(iota((PAIRS, HD), 0) == iota((PAIRS, HD), 1), total, 0.0), axis=0, keepdims=True)
    square_ref[...] = jnp.broadcast_to(line[None], square_ref.shape)


def merge(mixed, log, back, ways):
    return pl.pallas_call(
        merge_kernel,
        out_shape=(pltpu.VMEM((ROWS, HD), BF16), pltpu.VMEM((ways, 1, HD), F32)),
        in_specs=[VMEM] * 3,
        out_specs=(VMEM, VMEM),
        name="merge",
    )(*keep(mixed, log, back))


def norm_kernel(attn_ref, square_ref, gain_ref, out_ref):
    ways = square_ref.shape[0]
    line = square_ref[0]
    for i in range(1, ways):
        line = line + square_ref[i]
    line = jnp.broadcast_to(line, (PAIRS, HD))
    total = jnp.sum(jnp.where(iota((PAIRS, HD), 0) == iota((PAIRS, HD), 1), line, 0.0), axis=1, keepdims=True)
    scale = lax.rsqrt(total / (ways * HEADS * HD) + 1e-5)
    for h in range(HEADS):
        wide = attn_ref[h * PAIRS : (h + 1) * PAIRS, :].astype(F32)
        out = wide * scale * gain_ref[h : h + 1, :]
        for t in range(STEPS):
            out_ref[t, :, h * HD : (h + 1) * HD] = out[t * REQS : (t + 1) * REQS].astype(BF16)


def normalize(attn, square, gain):
    return pl.pallas_call(
        norm_kernel,
        out_shape=jax.ShapeDtypeStruct((STEPS, REQS, HEADS * HD), BF16),
        in_specs=[VMEM] * 3,
        out_specs=VMEM,
        name="normalize",
    )(*keep(attn, square, gain))


def body(
    lookup_vectors,
    fresh_token_memory,
    unfinished_block_memory,
    cache_block_store,
    sequence_block_index,
    sequence_history_count,
    unfinished_block_fill,
    migration_sender_block,
    migration_receiver_server,
    switch_moment,
    output_scaling_weights,
):
    ways = lax.axis_size("tp")
    core = (lax.axis_index("tp") & 1).astype(I32)
    replica = lax.axis_index("rep").astype(I32)
    half = (((replica >> 3) ^ ((replica >> 2) & (1 - core))) & 1).reshape(1)
    core = core.reshape(1)
    pool = cache_block_store.reshape(POOL, 2 * PAGE, HD)
    unfinished = unfinished_block_memory.reshape(REQS, 2 * PAGE, HD)
    fresh = fresh_token_memory.reshape(STEPS, REQS, 2, HD)
    gain = output_scaling_weights.reshape(HEADS, HD)
    fill, switch = unfinished_block_fill, switch_moment

    query = lookup_vectors.reshape(PAIRS, HEADS, HD)
    outgoing, request = send_tiles(
        half, core, migration_receiver_server.reshape(MIGS), migration_sender_block, sequence_history_count, fill, switch,
        pool, unfinished, fresh, query, sequence_block_index
    )
    tiles = lax.all_to_all(outgoing, ("rep", "tp"), split_axis=0, concat_axis=0, axis_index_groups=HALVES, tiled=True)
    tiles = tiles.reshape(PEERS, 4, 2 * PAGE, HD)

    asked = lax.ppermute(request, ("rep", "tp"), PARTNERS)
    pool_bias, near_bias = token_bias(("pool", "arrived"), half, core, request)
    mixed, log = local_part(fill, request, pool, unfinished, fresh, pool_bias)
    (far_bias,) = token_bias(("arrived",), half, core, asked)

    back = lax.ppermute(far_part(asked, far_bias, tiles, log), ("rep", "tp"), PARTNERS)
    mixed, log = near_part(request, near_bias, tiles, mixed, log)
    attn, square = merge(mixed, log, back, ways)
    square = lax.all_to_all(square, "tp", split_axis=0, concat_axis=0, axis_index_groups=SUMMED, tiled=True)
    return normalize(attn, square, gain)


def solution(mesh):
    rep = "rep"
    placed = (
        P(None, rep, "tp", None),
        P(None, rep, None, "tp", None),
        P(rep, None, None, "tp", None),
        P(rep, None, None, "tp", None),
        P(rep, None),
        P(rep),
        P(rep),
        P(rep),
        P(rep, None),
        P(rep),
        P("tp"),
    )
    return jax.shard_map(body, mesh=mesh, in_specs=placed, out_specs=P(None, rep, "tp"), check_vma=False)
```

```python
import jax
import jax.numpy as jnp
from jax import lax
from jax.experimental import pallas as pl
from jax.experimental.pallas import tpu as pltpu
from jax.sharding import PartitionSpec as P

STEPS, REQS, HEADS, HD = 4, 4, 16, 128
ROWS = STEPS * REQS * HEADS
PAIRS = STEPS * REQS
PAGE = 16
POOL = 64
MIGS = 64
PEERS = 32
TOKENS = POOL * PAGE
NEG = -1e30
MARK = 4096.0
SCALE = 1.4426950408889634 / HD**0.5
def place_of(member, core):
    if core == 1:
        return member ^ 18
    place = member ^ 18
    return ((place & 3) << 3) | (place & 4) | (place >> 3)


PLACES = [[place_of(j, core) for j in range(PEERS)] for core in range(2)]
ORDERS = [[places.index(k) for k in range(PEERS)] for places in PLACES]


def half_of(replica, core):
    half = (replica >> 3) & 1
    return half if core else half ^ ((replica >> 2) & 1)


def replica_of(member, half, core):
    zh = half if core else half ^ ((member >> 2) & 1)
    return ((member >> 3) << 4) | (zh << 3) | (member & 7)


def stand_of(target, core):
    far = half_of(target, core)
    image = target if core or not far else target ^ 4
    return PLACES[core][((image >> 4) << 3) | (image & 7)] * 4 + far * 2


HALVES = [[replica_of(j, half, tp % 2) * 8 + tp for j in ORDERS[tp % 2]] for half in range(2) for tp in range(8)]
STANDS = [stand_of(t, c) for c in range(2) for t in range(64)]
PARTNERS = [(p * 8 + tp, (p ^ (8 if tp % 2 else 4)) * 8 + tp) for p in range(64) for tp in range(8)]
SUMMED = [[4, 5, 2, 3, 6, 7, 0, 1]]
F32, BF16, I32 = jnp.float32, jnp.bfloat16, jnp.int32
VMEM = pl.BlockSpec(memory_space=pltpu.VMEM)
SMEM = pl.BlockSpec(memory_space=pltpu.SMEM)


def dot(a, b, ca, cb):
    return lax.dot_general(a, b, (((ca,), (cb,)), ((), ())), preferred_element_type=F32)


def iota(shape, axis):
    return lax.broadcasted_iota(I32, shape, axis)


def tail_tile(r, kv, fill, unfinished_ref, fresh_ref):
    rows = iota((PAGE, HD), 0)
    tile = unfinished_ref[r, kv * PAGE : (kv + 1) * PAGE, :].astype(F32)
    for s in range(STEPS):
        row = fresh_ref[s, r].astype(F32)[kv : kv + 1, :]
        tile = jnp.where(rows == fill + s, row, tile)
    return tile


def send_kernel(
    half_ref, core_ref, target_ref, source_ref, stand_ref, length_ref, fill_ref, switch_ref,
    pool_ref, unfinished_ref, fresh_ref, query_ref, table_ref, out_ref, request_ref, tiles_ref
):
    rows = iota((PAGE, HD), 0)
    blank = jnp.concatenate([jnp.full((PAGE, HD), MARK, BF16), jnp.zeros((PAGE, HD), BF16)], 0)
    out_ref[...] = jnp.broadcast_to(blank[None], out_ref.shape)
    tiles_ref[:POOL] = pool_ref[...]
    for r in range(REQS):
        fill = fill_ref[r]
        key = tail_tile(r, 0, fill, unfinished_ref, fresh_ref)
        value = tail_tile(r, 1, fill, unfinished_ref, fresh_ref)
        key = jnp.where(rows < fill + switch_ref[r], key, MARK)
        tiles_ref[POOL + r] = jnp.concatenate([key, value], 0).astype(BF16)
    flip = half_ref[0] * jnp.where(core_ref[0] == 1, 2, 2 + 4 * 4)
    table = core_ref[0] * 64
    low = jnp.int32(0)
    high = jnp.int32(0)
    for e in range(MIGS):
        t = target_ref[e]
        first = t < 32
        shift = t & 31
        word = jnp.where(first, low, high)
        rank = (word >> shift) & 1
        word = word | (jnp.int32(1) << shift)
        low = jnp.where(first, word, low)
        high = jnp.where(first, high, word)
        out_ref[(stand_ref[table + t] ^ flip) + rank] = tiles_ref[source_ref[e]]
    query = jnp.transpose(query_ref[...].astype(F32), (1, 0, 2))
    request_ref[:ROWS, :] = query.reshape(ROWS, HD).astype(BF16)
    row, lane = iota((16, HD), 0), iota((16, HD), 1)
    info = jnp.concatenate([table_ref[...], jnp.zeros((16 - REQS, HD), I32)], 0)
    for g in range(REQS):
        length = length_ref[g]
        at = row - REQS
        fact = jnp.where(at == 0, length >> 4, jnp.where(at == 1, length & 15, switch_ref[g]))
        info = jnp.where((lane == g) & (at >= 0) & (at < 3), fact, info)
    request_ref[ROWS:, :] = info.astype(F32).astype(BF16)


def keep(*arrays):
    return tuple(pltpu.with_memory_space_constraint(x, pltpu.VMEM) for x in arrays)


def send_tiles(half, core, target, source, length, fill, switch, pool, unfinished, fresh, query, table):
    return pl.pallas_call(
        send_kernel,
        out_shape=(pltpu.VMEM((PEERS * 4, 2 * PAGE, HD), BF16), pltpu.VMEM((ROWS + 16, HD), BF16)),
        in_specs=[SMEM] * 8 + [VMEM] * 5,
        out_specs=(VMEM, VMEM),
        scratch_shapes=[pltpu.VMEM((POOL + REQS, 2 * PAGE, HD), BF16)],
        cost_estimate=pl.CostEstimate(flops=1000, bytes_accessed=2**21, transcendentals=0),
        name="send_tiles",
    )(half, core, target, source, jnp.array(STANDS, I32), length, fill, switch, pool, unfinished, fresh, query, table)


def bias_kernel(sections, half_ref, core_ref, request_ref, *refs):
    info = request_ref[ROWS:, :].astype(F32).astype(I32)
    half = half_ref[0]
    token = iota((TOKENS, HD), 0)
    entry = iota((1, HD), 1)
    lane = iota((1, HD), 1)
    pair, part = lane % PAIRS, lane // PAIRS
    step, req = pair // REQS, pair % REQS
    held, weights = [], []
    late = jnp.zeros((1, HD), jnp.bool_)
    for g in range(REQS):
        pages, rest, moment = (info[REQS + i : REQS + i + 1, g : g + 1] for i in range(3))
        held.append(jnp.clip(pages * PAGE + rest - entry * PAGE, 0, PAGE).astype(jnp.uint32))
        late = late | ((req == g) & (step < moment))
        spread = iota((HD, HD), 1)
        weights.append(((spread % REQS == g) & (spread < 3 * PAIRS)).astype(BF16))
    weights = jnp.concatenate(weights, 0)
    for section, ref in zip(sections, refs, strict=True):
        spot = info[:REQS]
        if section != "pool":
            slot = spot - POOL
            peer = slot >> 1
            side = jnp.where(core_ref[0] == 1, half_of(peer, 1), half_of(peer, 0))
            here = (slot >= 0) & (side == half)
            peer = ((peer >> 4) << 3) | (peer & 7)
            peer = jnp.where(core_ref[0] == 1, place_of(peer, 1), place_of(peer, 0))
            spot = jnp.where(here, peer * 2 + (slot & 1), POOL)
        first = spot * PAGE
        hits = [
            jnp.where((token - first[g : g + 1, :]).astype(jnp.uint32) < held[g], 1.0, 0.0).astype(BF16) for g in range(REQS)
        ]
        count = dot(jnp.concatenate(hits, 1), weights, 1, 0)
        log = jnp.log2(jnp.maximum(count, 1.0)) * (1.0 / SCALE)
        high = log.astype(BF16).astype(F32)
        middle = (log - high).astype(BF16).astype(F32)
        parts = jnp.where(part == 0, high, jnp.where(part == 1, middle, log - high - middle))
        gone = count == 0
        if section != "pool":
            gone = gone | late
        ref[...] = jnp.where(gone, jnp.where(part == 0, NEG, 0.0), parts).astype(BF16)


def token_bias(sections, half, core, request):
    out = pltpu.VMEM((TOKENS, HD), BF16)
    return pl.pallas_call(
        lambda *refs: bias_kernel(sections, *refs),
        out_shape=(out,) * len(sections),
        in_specs=[SMEM, SMEM, VMEM],
        out_specs=(VMEM,) * len(sections),
        cost_estimate=pl.CostEstimate(flops=2**27, bytes_accessed=2**18, transcendentals=0),
        name="token_bias",
    )(half, core, *keep(request))


def attend(query, key, value, bias):
    lane, row = iota((ROWS, HD), 1), iota((ROWS, HD), 0)
    reads = ((lane % PAIRS == row % PAIRS) & (lane < 3 * PAIRS)).astype(BF16)
    scores = dot(jnp.concatenate([query, reads], 1), jnp.concatenate([key, bias], 1), 1, 1)
    top = jnp.max(scores, axis=-1, keepdims=True)
    probs = jnp.exp2((scores - top) * SCALE).astype(BF16)
    mixed = dot(probs, jnp.concatenate([value, jnp.ones(value.shape, BF16)], 1), 1, 0)
    total = mixed[:, HD:]
    return mixed[:, :HD] / total, top * SCALE + jnp.log2(total)


def combine(a, b):
    (x, p), (y, q) = a, b
    top = jnp.maximum(p, q)
    u, v = jnp.exp2(p - top), jnp.exp2(q - top)
    return (x * u + y * v) / (u + v), top + jnp.log2(u + v)


def local_kernel(fill_ref, request_ref, pool_ref, unfinished_ref, fresh_ref, bias_ref, mixed_ref, log_ref):
    tail = 2 * REQS * PAGE
    keys = [pool_ref[:, :PAGE, :].reshape(TOKENS, HD)]
    values = [pool_ref[:, PAGE:, :].reshape(TOKENS, HD)]
    token, lane = iota((tail, HD), 0), iota((tail, HD), 1)
    step, req = lane % PAIRS // REQS, lane % REQS
    held = jnp.zeros((tail, HD), I32)
    for r in range(REQS):
        fill = fill_ref[r]
        keys.append(tail_tile(r, 0, fill, unfinished_ref, fresh_ref).astype(BF16))
        values.append(tail_tile(r, 1, fill, unfinished_ref, fresh_ref).astype(BF16))
        held = jnp.where(req == r, fill, held)
    keys.append(jnp.zeros((tail // 2, HD), BF16))
    values.append(jnp.zeros((tail // 2, HD), BF16))
    valid = (token // PAGE == req) & (token % PAGE < held + step + 1)
    bias = jnp.where((lane >= PAIRS) | valid, 0.0, NEG).astype(BF16)
    bias = jnp.concatenate([bias_ref[...], bias], 0)
    mixed, log = attend(request_ref[:ROWS, :], jnp.concatenate(keys, 0), jnp.concatenate(values, 0), bias)
    mixed_ref[...] = mixed
    log_ref[...] = log


def local_part(fill, request, pool, unfinished, fresh, bias):
    out = pltpu.VMEM((ROWS, HD), F32)
    request, bias = keep(request, bias)
    return pl.pallas_call(
        local_kernel,
        out_shape=(out, out),
        in_specs=[SMEM] + [VMEM] * 5,
        out_specs=(VMEM, VMEM),
        cost_estimate=pl.CostEstimate(flops=2**28, bytes_accessed=2**20, transcendentals=2**18),
        name="local_part",
    )(fill, request, pool, unfinished, fresh, bias)


def arrived_part(request_ref, bias_ref, tiles_ref, which):
    tiles = tiles_ref[:, 2 * which : 2 * which + 2]
    key = tiles[:, :, :PAGE, :].reshape(TOKENS, HD)
    value = tiles[:, :, PAGE:, :].reshape(TOKENS, HD)
    bias = jnp.where(key > MARK / 2, jnp.asarray(NEG, BF16), bias_ref[...])
    return attend(request_ref[:ROWS, :], key, value, bias)


def far_kernel(request_ref, bias_ref, tiles_ref, after_ref, out_ref):
    mixed, log = arrived_part(request_ref, bias_ref, tiles_ref, 1)
    out_ref[:ROWS, :] = mixed.astype(BF16)
    lane = iota((ROWS, HD), 1)
    high = log.astype(BF16).astype(F32)
    middle = (log - high).astype(BF16).astype(F32)
    least = log - high - middle
    parts = jnp.where(lane == 0, high, jnp.where(lane == 1, middle, jnp.where(lane == 2, least, 0.0)))
    eye = (iota((8, HD), 0) == iota((8, HD), 1)).astype(BF16)
    across = dot(eye, parts.astype(BF16), 1, 1)
    out_ref[ROWS:, :] = jnp.concatenate([across[:, :HD], across[:, HD:]], 0).astype(BF16)


def far_part(request, bias, tiles, after):
    return pl.pallas_call(
        far_kernel,
        out_shape=pltpu.VMEM((ROWS + 16, HD), BF16),
        in_specs=[VMEM] * 3 + [pl.BlockSpec(memory_space=pl.ANY)],
        out_specs=VMEM,
        cost_estimate=pl.CostEstimate(flops=2**28, bytes_accessed=2**20, transcendentals=2**18),
        name="far_part",
    )(*keep(request, bias, tiles, after))


def near_kernel(request_ref, bias_ref, tiles_ref, mixed_ref, log_ref, out_ref, sum_ref):
    part = arrived_part(request_ref, bias_ref, tiles_ref, 0)
    mixed, log = combine((mixed_ref[...], log_ref[...]), part)
    out_ref[...] = mixed
    sum_ref[...] = log


def near_part(request, bias, tiles, mixed, log):
    out = pltpu.VMEM((ROWS, HD), F32)
    return pl.pallas_call(
        near_kernel,
        out_shape=(out, out),
        in_specs=[VMEM] * 5,
        out_specs=(VMEM, VMEM),
        cost_estimate=pl.CostEstimate(flops=2**28, bytes_accessed=2**20, transcendentals=2**18),
        name="near_part",
    )(*keep(request, bias, tiles, mixed, log))


def merge_kernel(mixed_ref, log_ref, back_ref, attn_ref, square_ref):
    stats = back_ref[ROWS:, :].astype(F32)
    stats = jnp.concatenate([stats[:8], stats[8:]], 1).astype(BF16)
    log = dot(stats, jnp.ones((8, HD), BF16), 0, 0)
    mixed, _ = combine((mixed_ref[...], log_ref[...]), (back_ref[:ROWS, :].astype(F32), log))
    attn = mixed.astype(BF16)
    attn_ref[...] = attn
    wide = attn.astype(F32)
    square = wide * wide
    total = square[:PAIRS]
    for h in range(1, HEADS):
        total = total + square[h * PAIRS : (h + 1) * PAIRS]
    total = jnp.sum(total, axis=-1, keepdims=True)
    line = jnp.sum(jnp.where(iota((PAIRS, HD), 0) == iota((PAIRS, HD), 1), total, 0.0), axis=0, keepdims=True)
    square_ref[...] = jnp.broadcast_to(line[None], square_ref.shape)


def merge(mixed, log, back, ways):
    return pl.pallas_call(
        merge_kernel,
        out_shape=(pltpu.VMEM((ROWS, HD), BF16), pltpu.VMEM((ways, 1, HD), F32)),
        in_specs=[VMEM] * 3,
        out_specs=(VMEM, VMEM),
        name="merge",
    )(*keep(mixed, log, back))


def norm_kernel(attn_ref, square_ref, gain_ref, out_ref):
    ways = square_ref.shape[0]
    line = square_ref[0]
    for i in range(1, ways):
        line = line + square_ref[i]
    line = jnp.broadcast_to(line, (PAIRS, HD))
    total = jnp.sum(jnp.where(iota((PAIRS, HD), 0) == iota((PAIRS, HD), 1), line, 0.0), axis=1, keepdims=True)
    scale = lax.rsqrt(total / (ways * HEADS * HD) + 1e-5)
    for h in range(HEADS):
        wide = attn_ref[h * PAIRS : (h + 1) * PAIRS, :].astype(F32)
        out = wide * scale * gain_ref[h : h + 1, :]
        for t in range(STEPS):
            out_ref[t, :, h * HD : (h + 1) * HD] = out[t * REQS : (t + 1) * REQS].astype(BF16)


def normalize(attn, square, gain):
    return pl.pallas_call(
        norm_kernel,
        out_shape=jax.ShapeDtypeStruct((STEPS, REQS, HEADS * HD), BF16),
        in_specs=[VMEM] * 3,
        out_specs=VMEM,
        name="normalize",
    )(*keep(attn, square, gain))


def body(
    lookup_vectors,
    fresh_token_memory,
    unfinished_block_memory,
    cache_block_store,
    sequence_block_index,
    sequence_history_count,
    unfinished_block_fill,
    migration_sender_block,
    migration_receiver_server,
    switch_moment,
    output_scaling_weights,
):
    ways = lax.axis_size("tp")
    core = (lax.axis_index("tp") & 1).astype(I32)
    replica = lax.axis_index("rep").astype(I32)
    half = (((replica >> 3) ^ ((replica >> 2) & (1 - core))) & 1).reshape(1)
    core = core.reshape(1)
    pool = cache_block_store.reshape(POOL, 2 * PAGE, HD)
    unfinished = unfinished_block_memory.reshape(REQS, 2 * PAGE, HD)
    fresh = fresh_token_memory.reshape(STEPS, REQS, 2, HD)
    gain = output_scaling_weights.reshape(HEADS, HD)
    fill, switch = unfinished_block_fill, switch_moment

    query = lookup_vectors.reshape(PAIRS, HEADS, HD)
    outgoing, request = send_tiles(
        half, core, migration_receiver_server.reshape(MIGS), migration_sender_block, sequence_history_count, fill, switch,
        pool, unfinished, fresh, query, sequence_block_index
    )
    tiles = lax.all_to_all(outgoing, ("rep", "tp"), split_axis=0, concat_axis=0, axis_index_groups=HALVES, tiled=True)
    tiles = tiles.reshape(PEERS, 4, 2 * PAGE, HD)

    asked = lax.ppermute(request, ("rep", "tp"), PARTNERS)
    pool_bias, near_bias = token_bias(("pool", "arrived"), half, core, request)
    mixed, log = local_part(fill, request, pool, unfinished, fresh, pool_bias)
    (far_bias,) = token_bias(("arrived",), half, core, asked)

    back = lax.ppermute(far_part(asked, far_bias, tiles, log), ("rep", "tp"), PARTNERS)
    mixed, log = near_part(request, near_bias, tiles, mixed, log)
    attn, square = merge(mixed, log, back, ways)
    square = lax.all_to_all(square, "tp", split_axis=0, concat_axis=0, axis_index_groups=SUMMED, tiled=True)
    return normalize(attn, square, gain)


def solution(mesh):
    rep = "rep"
    placed = (
        P(None, rep, "tp", None),
        P(None, rep, None, "tp", None),
        P(rep, None, None, "tp", None),
        P(rep, None, None, "tp", None),
        P(rep, None),
        P(rep),
        P(rep),
        P(rep),
        P(rep, None),
        P(rep),
        P("tp"),
    )
    return jax.shard_map(body, mesh=mesh, in_specs=placed, out_specs=P(None, rep, "tp"), check_vma=False)
```
